128 devices in a mesh: ctx: 16 (over y, x), ch: 8 (over z, core).
Axes of the slice: x: 4, y: 4, z: 4, core: 2. Of those that a mesh axis runs over, the one named last changes fastest.
Arguments:
- query: bfloat16 [8192, 8192], P('ctx', 'ch'), may hold values from -6 to 6
- keys_in: bfloat16 [8192, 8192], P('ctx', 'ch'), may hold values from -6 to 6
- values_in: bfloat16 [8192, 8192], P('ctx', 'ch'), may hold values from -6 to 6
- short_taps: float32 [3, 3, 8192], P(None, None, 'ch'), may hold values from -3.5 to 3.5
- mode_rates: float32 [16, 8192], P(None, 'ch'), may hold values from 0.00012207031 to 0.05
- mode_residues: float32 [16, 8192], P(None, 'ch'), may hold values from -0.06629126 to 0.06629126
- out_weight: bfloat16 [8192, 8192], P('ctx', 'ch'), may hold values from -0.0625 to 0.0625
Outputs:
- mixed: bfloat16 [8192, 8192], P('ctx', 'ch')
The draws below stay inside these ranges and needn't reach their ends.
All inputs are finite; a program needn't handle non-finite values.
Results may differ from the reference program's by a relative error of at most 0.018.
Values may be sent and summed in bfloat16 or wider, within the bound.
A program may use at most 128 MiB of HBM per device.

```python
import math
import jax
import jax.numpy as jnp
from jax import lax

D = 8192
TAPS = 3
ORDER = 16
SEQ = 8192


def levels(own_key, extent, cuts, smallest, high):
    def one(position, parts):
        heights = jax.random.uniform(jax.random.fold_in(jax.random.fold_in(own_key, 6), position), (parts,), jnp.float32, smallest / len(cuts), high / len(cuts))
        return jnp.repeat(jnp.exp(heights), extent[position] // parts).reshape((-1,) + (1,) * (len(extent) - position - 1))

    factor_of = one(*cuts[0])
    for cut in cuts[1:]:
        factor_of = factor_of * one(*cut)
    return factor_of


def normal_values(stream_key, dims, deviation, most, cuts=(), kind=jnp.bfloat16):
    drawn = deviation * jax.random.normal(stream_key, dims, jnp.float32)
    if cuts:
        drawn = drawn * levels(stream_key, dims, cuts, -0.22, 0.18)
    return jnp.clip(drawn, -most, most).astype(kind)


def setup_inputs(seed: int = 0) -> dict:
    seeds = jax.random.split(jax.random.key(seed), 8)
    query = normal_values(seeds[0], (SEQ, D), 1.0, 6.0, ((0, 16), (1, 8)))
    keys_in = normal_values(seeds[1], (SEQ, D), 1.0, 6.0, ((0, 16), (1, 8)))
    values_in = normal_values(seeds[2], (SEQ, D), 1.0, 6.0, ((0, 16), (1, 8)))
    short_taps = normal_values(seeds[3], (3, TAPS, D), TAPS ** -0.5, 3.5, ((2, 8),), jnp.float32)
    mode_rates = jnp.clip(jnp.exp(math.log(0.05) - 6.015181 * jax.random.uniform(seeds[4], (ORDER, D), jnp.float32) ** levels(seeds[4], (ORDER, D), ((1, 8),), -0.2, 0.2)), 0.00012207031, 0.05)
    mode_residues = normal_values(seeds[5], (ORDER, D), (4.0 / (ORDER * SEQ) ** 0.5), 0.06629126, ((1, 8),), jnp.float32)
    out_weight = normal_values(seeds[6], (D, D), D ** -0.5, 0.0625, ((0, 16), (1, 8)))
    return {"query": query, "keys_in": keys_in, "values_in": values_in, "short_taps": short_taps, "mode_rates": mode_rates, "mode_residues": mode_residues, "out_weight": out_weight}


def depthwise(padded, taps_block):
    channels = padded.shape[1]
    kernel = taps_block[::-1][:, None, :]
    result = lax.conv_general_dilated(padded[None], kernel, (1,), "VALID", dimension_numbers=("NWC", "WIO", "NWC"), feature_group_count=channels, precision=lax.Precision.HIGHEST)
    return result[0]


def reference(query, keys_in, values_in, short_taps, mode_rates, mode_residues, out_weight):
    length = query.shape[0]
    channels = query.shape[1]
    group = math.gcd(channels, 512)
    group_count = channels // group

    def per_group(number):
        start = (number * group).astype(jnp.int32)

        def take(array):
            return lax.dynamic_slice_in_dim(array, start, group, array.ndim - 1)

        taps_here = take(short_taps)

        def featurize(stream, index):
            padded = jnp.pad(take(stream).astype(jnp.float32), ((TAPS - 1, 0), (0, 0)))
            return depthwise(padded, taps_here[index]).astype(jnp.bfloat16)

        qf = featurize(query, 0)
        kf = featurize(keys_in, 1)
        vf = featurize(values_in, 2)
        gated = (kf.astype(jnp.float32) * vf.astype(jnp.float32)).astype(jnp.bfloat16)
        rates = take(mode_rates)
        residues = take(mode_residues)
        positions = jnp.arange(length, dtype=jnp.float32)
        kernel = jnp.zeros((length, group), jnp.float32)
        for mode in range(ORDER):
            kernel = kernel + residues[mode][None, :] * jnp.exp(-positions[:, None] * rates[mode][None, :])
        spectrum = jnp.fft.rfft(gated.astype(jnp.float32), n=2 * length, axis=0) * jnp.fft.rfft(kernel, n=2 * length, axis=0)
        longconv = jnp.fft.irfft(spectrum, n=2 * length, axis=0)[:length]
        return (qf.astype(jnp.float32) * longconv).astype(jnp.bfloat16)

    blocks = lax.map(per_group, jnp.arange(group_count, dtype=jnp.int32))
    output = blocks.transpose(1, 0, 2).reshape(length, channels)
    mixed = jnp.dot(output.astype(jnp.float32), out_weight.astype(jnp.float32), precision=lax.Precision.HIGHEST)
    return mixed.astype(jnp.bfloat16)
```

```python
import functools

import jax
import jax.numpy as jnp
from jax import lax
from jax.experimental import pallas as pl
from jax.experimental.pallas import tpu as pltpu
from jax.sharding import PartitionSpec as P

MESH = pl.DeviceIdType.MESH
SIDE = 4
ORDER = 16
ROWS = 512
WIDTH = 1024
LANES = 128
TILES = WIDTH // LANES
SEGS = 8
STEPS = ROWS // SEGS
HALF = ROWS // 2
QUART = ROWS // 4
PAD = 8
HALO = 16
OFFS = (0, -1, 1, 2)
F32 = jnp.float32
BF16 = jnp.bfloat16


def rounded(value):
    return value.astype(BF16).astype(F32)


def kernel(
    q_ref, k_ref, v_ref, taps_ref, rates_ref, res_ref, w_ref, out_ref,
    wbuf, abuf, acc, streams, gbuf, ybuf, halo, dec, ends, inits, xstate, ystate,
    w_send, w_recv, a_send, a_recv, h_send, h_recv, s_send, s_recv, own_sem,
):
    ctx = lax.axis_index("ctx")
    ch = lax.axis_index("ch")
    cy, cx = ctx // SIDE, ctx % SIDE
    cz, core = ch // 2, ch % 2

    def mod(value):
        return lax.rem(value + 2 * SIDE, SIDE)

    def at_xy(y, x):
        return (mod(y) * SIDE + mod(x), ch)

    following = (lax.rem(ctx + 1, SIDE * SIDE), ch)
    previous = (lax.rem(ctx + SIDE * SIDE - 1, SIDE * SIDE), ch)
    sibling = (ctx, cz * 2 + 1 - core)

    def at_z(z):
        return (ctx, mod(z) * 2 + core)

    barrier = pltpu.get_barrier_semaphore()
    partners = [at_xy(cy, cx + d) for d in (1, 2, 3)] + [at_xy(cy + d, cx) for d in (1, 2, 3)]
    partners += [at_z(cz + 1), at_z(cz - 1), sibling, following, previous]
    for partner in partners:
        pl.semaphore_signal(barrier, inc=1, device_id=partner, device_id_type=MESH)

    own_copy = pltpu.make_async_copy(w_ref, wbuf.at[ctx], own_sem)
    own_copy.start()
    own_copy.wait()
    pl.semaphore_wait(barrier, len(partners))

    def halo_copy(index):
        source = (q_ref, k_ref, v_ref)[index]
        return pltpu.make_async_remote_copy(
            src_ref=source.at[pl.ds(ROWS - HALO, HALO)], dst_ref=halo.at[index],
            send_sem=h_send.at[index], recv_sem=h_recv.at[index],
            device_id=following, device_id_type=MESH)

    for index in (1, 2, 0):
        halo_copy(index).start()

    def slot(half, first, second):
        first, second = mod(first), mod(second)
        return second * SIDE + first if half == 0 else first * SIDE + second

    mine = ((cx, cy), (cy, cx))

    def device_of(half, first, second):
        return at_xy(second, first) if half == 0 else at_xy(first, second)

    def w_copy(half, stage, piece, kind, receiving):
        f0, s0 = mine[half]
        f, s = f0, s0
        if stage == 1:
            f = f0 + OFFS[piece]
        step = 1 if kind % 2 == 0 else -1
        if receiving:
            back = -step if kind < 2 else -2 * step
        else:
            back = 0 if kind < 2 else -step
        if stage == 0:
            f = f + back
            target = device_of(half, f0 + step, s0)
        else:
            s = s + back
            target = device_of(half, f0, s0 + step)
        start = half * HALF + (QUART if kind == 3 else 0)
        size = HALF if kind < 2 else QUART
        where = wbuf.at[slot(half, f, s), pl.ds(start, size)]
        index = half * 20 + (kind if stage == 0 else 4 + 4 * piece + kind)
        return pltpu.make_async_remote_copy(
            src_ref=where, dst_ref=where, send_sem=w_send.at[index], recv_sem=w_recv.at[index],
            device_id=target, device_id_type=MESH)

    def w_start(half, stage, piece, kind):
        w_copy(half, stage, piece, kind, False).start()

    def w_wait(half, stage, piece, kind):
        w_copy(half, stage, piece, kind, True).wait_recv()

    def w_own(stage):
        for half in (0, 1):
            for kind in (0, 1):
                w_start(half, stage, 0, kind)

    def w_first():
        for half in (0, 1):
            for kind in (0, 1):
                w_wait(half, 0, 0, kind)
                w_start(half, 0, 0, kind + 2)
                w_start(half, 1, kind + 1, 0)
                w_start(half, 1, kind + 1, 1)

    def w_second(piece):
        for half in (0, 1):
            for kind in (0, 1):
                w_wait(half, 1, piece, kind)
                w_start(half, 1, piece, kind + 2)

    def w_opposite():
        for half in (0, 1):
            for kind in (2, 3):
                w_wait(half, 0, 0, kind)
            w_start(half, 1, 3, 0)
            w_start(half, 1, 3, 1)

    def w_last(piece):
        for half in (0, 1):
            for kind in (2, 3):
                w_wait(half, 1, piece, kind)

    def a_copy(kind, receiving):
        start, size = 0, ROWS
        if kind < 4:
            step = 1 if kind % 2 == 0 else -1
            if receiving:
                back = -step if kind < 2 else -2 * step
            else:
                back = 0 if kind < 2 else -step
            if kind >= 2:
                start, size = (HALF if kind == 3 else 0), HALF
            block = mod(cz + back) * 2 + core
            target = at_z(cz + step)
        else:
            side = 1 - core if receiving else core
            block = mod(cz + OFFS[kind - 4]) * 2 + side
            target = sibling
        where = abuf.at[block, pl.ds(start, size)]
        return pltpu.make_async_remote_copy(
            src_ref=where, dst_ref=where, send_sem=a_send.at[kind], recv_sem=a_recv.at[kind],
            device_id=target, device_id_type=MESH)

    def state_copy(stage, distance, receiving):
        held = (xstate, ystate)[stage]
        position = (cx, cy)[stage]
        index = mod(position - distance) if receiving else position
        target = at_xy(cy, cx + distance) if stage == 0 else at_xy(cy + distance, cx)
        number = stage * 3 + distance - 1
        return pltpu.make_async_remote_copy(
            src_ref=held.at[index], dst_ref=held.at[index],
            send_sem=s_send.at[number], recv_sem=s_recv.at[number],
            device_id=target, device_id_type=MESH)

    w_own(0)
    w_own(1)

    dec[...] = jnp.exp(-rates_ref[...])

    def widen(index):
        source = (q_ref, k_ref, v_ref)[index]

        def body(tile, carry):
            lanes = pl.ds(pl.multiple_of(tile * LANES, LANES), LANES)
            streams[index, tile, pl.ds(PAD, ROWS), :] = source[:, lanes].astype(F32)
            return carry

        lax.fori_loop(0, TILES, body, 0)

    def widen_halo(index):
        halo_copy(index).wait_recv()
        keep = jnp.where(ctx > 0, 1.0, 0.0).astype(F32)

        def body(tile, carry):
            lanes = pl.ds(pl.multiple_of(tile * LANES, LANES), LANES)
            rim = halo[index, :, lanes].astype(F32)
            streams[index, tile, pl.ds(0, PAD), :] = rim[HALO - PAD:] * keep
            return carry

        lax.fori_loop(0, TILES, body, 0)

    widen(1)
    widen(2)
    widen(0)
    widen_halo(1)
    widen_halo(2)
    widen_halo(0)

    def spread(row):
        return jnp.broadcast_to(row, (SEGS, LANES))

    def strided(index, tile, start):
        return streams[index, tile, pl.ds(start, SEGS, stride=STEPS), :]

    def tap_rows(index, lanes):
        return [spread(taps_ref[pl.ds(index * 3 + j, 1), lanes]) for j in range(3)]

    def first_tile(tile, carry):
        lanes = pl.ds(pl.multiple_of(tile * LANES, LANES), LANES)
        decay = [spread(dec[pl.ds(r, 1), lanes]) for r in range(ORDER)]
        k_taps, v_taps = tap_rows(1, lanes), tap_rows(2, lanes)

        def step(i, held):
            k1, k2, v1, v2, states = held
            k0, v0 = strided(1, tile, PAD + i), strided(2, tile, PAD + i)
            kf = rounded(k_taps[0] * k0 + k_taps[1] * k1 + k_taps[2] * k2)
            vf = rounded(v_taps[0] * v0 + v_taps[1] * v1 + v_taps[2] * v2)
            gated = rounded(kf * vf)
            gbuf[tile, i] = gated
            states = tuple(decay[r] * states[r] + gated for r in range(ORDER))
            return k0, k1, v0, v1, states

        zero = jnp.zeros((SEGS, LANES), F32)
        start = (strided(1, tile, PAD - 1), strided(1, tile, PAD - 2),
                 strided(2, tile, PAD - 1), strided(2, tile, PAD - 2), (zero,) * ORDER)
        states = lax.fori_loop(0, STEPS, step, start, unroll=2)[4]
        for r in range(ORDER):
            ends[tile, pl.ds(r, SEGS, stride=ORDER), :] = states[r]
        return carry

    lax.fori_loop(0, TILES, first_tile, 0)

    def combine_tile(tile, carry):
        lanes = pl.ds(pl.multiple_of(tile * LANES, LANES), LANES)
        jump = jnp.exp(-float(STEPS) * rates_ref[:, lanes])
        state = jnp.zeros((ORDER, LANES), F32)
        for seg in range(SEGS):
            inits[tile, pl.ds(seg * ORDER, ORDER), :] = state
            state = jump * state + ends[tile, pl.ds(seg * ORDER, ORDER), :]
        xstate[cx, :, lanes] = state
        return carry

    lax.fori_loop(0, TILES, combine_tile, 0)
    for distance in (1, 3, 2):
        state_copy(0, distance, False).start()

    w_first()

    for distance in (1, 3, 2):
        state_copy(0, distance, True).wait_recv()

    def row_tile(tile, carry):
        lanes = pl.ds(pl.multiple_of(tile * LANES, LANES), LANES)
        jump = jnp.exp(-float(ROWS) * rates_ref[:, lanes])
        state = jnp.zeros((ORDER, LANES), F32)
        for position in range(SIDE):
            state = jump * state + xstate[position, :, lanes]
        ystate[cy, :, lanes] = state
        return carry

    lax.fori_loop(0, TILES, row_tile, 0)
    for distance in (1, 3, 2):
        state_copy(1, distance, False).start()

    w_second(0)

    for distance in (1, 3, 2):
        state_copy(1, distance, True).wait_recv()

    def seed_tile(tile, carry):
        lanes = pl.ds(pl.multiple_of(tile * LANES, LANES), LANES)
        rate = rates_ref[:, lanes]
        jump_x = jnp.exp(-float(ROWS) * rate)
        jump_y = jnp.exp(-float(ROWS * SIDE) * rate)
        before_x = jnp.zeros((ORDER, LANES), F32)
        before_y = jnp.zeros((ORDER, LANES), F32)
        for position in range(SIDE - 1):
            before_x = jnp.where(position < cx, jump_x * before_x + xstate[position, :, lanes], before_x)
            before_y = jnp.where(position < cy, jump_y * before_y + ystate[position, :, lanes], before_y)
        shift = (cx * ROWS).astype(F32)
        state = before_x + jnp.exp(-shift * rate) * before_y
        jump = jnp.exp(-float(STEPS) * rate)
        for seg in range(SEGS):
            rows = pl.ds(seg * ORDER, ORDER)
            inits[tile, rows, :] = inits[tile, rows, :] + state
            state = jump * state
        return carry

    lax.fori_loop(0, TILES, seed_tile, 0)

    def second_tile(tile, carry):
        lanes = pl.ds(pl.multiple_of(tile * LANES, LANES), LANES)
        decay = [spread(dec[pl.ds(r, 1), lanes]) for r in range(ORDER)]
        weight = [spread(res_ref[pl.ds(r, 1), lanes]) for r in range(ORDER)]
        q_taps = tap_rows(0, lanes)

        def step(i, held):
            q1, q2, states = held
            q0 = strided(0, tile, PAD + i)
            qf = rounded(q_taps[0] * q0 + q_taps[1] * q1 + q_taps[2] * q2)
            gated = gbuf[tile, i]
            states = tuple(decay[r] * states[r] + gated for r in range(ORDER))
            terms = [weight[r] * states[r] for r in range(ORDER)]
            while len(terms) > 1:
                terms = [terms[j] + terms[j + 1] for j in range(0, len(terms), 2)]
            ybuf[pl.ds(i, SEGS, stride=STEPS), :] = qf * terms[0]
            return q0, q1, states

        start = (strided(0, tile, PAD - 1), strided(0, tile, PAD - 2),
                 tuple(inits[tile, pl.ds(r, SEGS, stride=ORDER), :] for r in range(ORDER)))
        lax.fori_loop(0, STEPS, step, start, unroll=2)
        abuf[ch, :, lanes] = ybuf[...].astype(BF16)
        return carry

    lax.fori_loop(0, TILES, second_tile, 0)

    for kind in (0, 1, 4):
        a_copy(kind, False).start()

    w_opposite()
    w_last(0)

    for kind in (0, 1):
        a_copy(kind, True).wait_recv()
        a_copy(kind + 2, False).start()
        a_copy(kind + 5, False).start()

    w_second(1)
    w_second(2)

    for kind in (2, 3):
        a_copy(kind, True).wait_recv()
    a_copy(7, False).start()
    acc[...] = jnp.zeros_like(acc)
    for kind in (4, 5, 6, 7):
        a_copy(kind, True).wait_recv()

    def multiply(dy, dx):
        y, x = mod(cy + dy), mod(cx + dx)
        shard = y * SIDE + x
        block = shard // 2
        columns = pl.ds(pl.multiple_of((shard % 2) * ROWS, ROWS), ROWS)

        def body(chunk, carry):
            lanes = pl.ds(pl.multiple_of(chunk * HALF, HALF), HALF)
            acc[:, lanes] += jnp.dot(
                abuf[block, :, columns], wbuf[shard, :, lanes], preferred_element_type=F32)
            return carry

        lax.fori_loop(0, WIDTH // HALF, body, 0)

    def near(t, carry):
        multiply(t // 3 - 1, t % 3 - 1)
        return carry

    lax.fori_loop(0, 9, near, 0)

    w_second(3)

    def straight(t, carry):
        multiply(2 * t, 2 - 2 * t)
        return carry

    lax.fori_loop(0, 2, straight, 0)

    w_last(1)
    w_last(2)

    def slanted(t, carry):
        across = t // 2
        sign = 2 * (t % 2) - 1
        multiply(2 * across + sign * (1 - across), 2 * (1 - across) + sign * across)
        return carry

    lax.fori_loop(0, 4, slanted, 0)

    w_last(3)

    def final(t, carry):
        multiply(2 + t, 2)
        return carry

    lax.fori_loop(0, 1, final, 0)
    out_ref[...] = acc[...].astype(BF16)

    for half in (0, 1):
        for kind in range(4):
            w_copy(half, 0, 0, kind, False).wait_send()
            for piece in range(4):
                w_copy(half, 1, piece, kind, False).wait_send()
    for kind in range(8):
        a_copy(kind, False).wait_send()
    for index in range(3):
        halo_copy(index).wait_send()
    for stage in range(2):
        for distance in (1, 2, 3):
            state_copy(stage, distance, False).wait_send()


def per_device(query, keys_in, values_in, short_taps, mode_rates, mode_residues, out_weight):
    vmem = pl.BlockSpec(memory_space=pltpu.VMEM)
    dma = pltpu.SemaphoreType.DMA
    return pl.pallas_call(
        kernel,
        out_shape=jax.ShapeDtypeStruct((ROWS, WIDTH), BF16),
        in_specs=[vmem] * 6 + [pl.BlockSpec(memory_space=pl.ANY)],
        out_specs=vmem,
        scratch_shapes=[
            pltpu.VMEM((SIDE * SIDE, ROWS, WIDTH), BF16),
            pltpu.VMEM((8, ROWS, WIDTH), BF16),
            pltpu.VMEM((ROWS, WIDTH), F32),
            pltpu.VMEM((3, TILES, PAD + ROWS, LANES), F32),
            pltpu.VMEM((TILES, STEPS, SEGS, LANES), F32),
            pltpu.VMEM((ROWS, LANES), F32),
            pltpu.VMEM((3, HALO, WIDTH), BF16),
            pltpu.VMEM((ORDER, WIDTH), F32),
            pltpu.VMEM((TILES, SEGS * ORDER, LANES), F32),
            pltpu.VMEM((TILES, SEGS * ORDER, LANES), F32),
            pltpu.VMEM((SIDE, ORDER, WIDTH), F32),
            pltpu.VMEM((SIDE, ORDER, WIDTH), F32),
            dma((40,)), dma((40,)), dma((8,)), dma((8,)), dma((3,)), dma((3,)), dma((6,)), dma((6,)),
            dma,
        ],
        compiler_params=pltpu.CompilerParams(
            collective_id=0, has_side_effects=True, vmem_limit_bytes=56 * 1024 * 1024),
        cost_estimate=pl.CostEstimate(
            flops=2 * ROWS * 8192 * WIDTH, bytes_accessed=6 * 1024 * 1024, transcendentals=0),
    )(query, keys_in, values_in, short_taps.reshape(9, WIDTH), mode_rates, mode_residues, out_weight)


def solution(mesh):
    in_specs = (
        P("ctx", "ch"),
        P("ctx", "ch"),
        P("ctx", "ch"),
        P(None, None, "ch"),
        P(None, "ch"),
        P(None, "ch"),
        P("ctx", "ch"),
    )
    return jax.shard_map(
        per_device, mesh=mesh, in_specs=in_specs, out_specs=P("ctx", "ch"), check_vma=False
    )
```

```python
import jax
import jax.numpy as jnp
from jax import lax
from jax.experimental import pallas as pl
from jax.experimental.pallas import tpu as pltpu
from jax.sharding import PartitionSpec as P

MESH = pl.DeviceIdType.MESH
SIDE = 4
ORDER = 16
ROWS = 512
WIDTH = 1024
LANES = 128
TILES = WIDTH // LANES
SEGS = 8
STEPS = ROWS // SEGS
PAD = 8
HALO = 16
PARTS = 2
PART = WIDTH // PARTS
CHUNKS = 4
CHUNK = WIDTH // CHUNKS
CUT = 224
OFFS = (0, -1, 1, 2)
PER_CHUNK = 17
F32 = jnp.float32
BF16 = jnp.bfloat16


def rounded(value):
    return value.astype(BF16).astype(F32)


def kernel(
    q_hbm, k_hbm, v_hbm, taps_ref, rates_ref, res_ref, w_ref, out_ref,
    wbuf, abuf, acc, cout, cin, inputs, streams, gbuf, ybuf, halo, dec, ends, inits, xstate, ystate,
    w_send, w_recv, a_send, a_recv, p_send, p_recv, c_send, c_recv, h_send, h_recv, s_send, s_recv,
    own_sem, in_sem,
):
    ctx = lax.axis_index("ctx")
    ch = lax.axis_index("ch")
    cy, cx = ctx // SIDE, ctx % SIDE
    cz, core = ch // 2, ch % 2
    column, side = cx % 2, cx // 2
    role = jnp.where(core == side, 0, 1)

    def mod(value):
        return lax.rem(value + 2 * SIDE, SIDE)

    def at_xy(y, x):
        return (mod(y) * SIDE + mod(x), ch)

    following = (lax.rem(ctx + 1, SIDE * SIDE), ch)
    previous = (lax.rem(ctx + SIDE * SIDE - 1, SIDE * SIDE), ch)
    sibling = (ctx, cz * 2 + 1 - core)
    beside = at_xy(cy, cx + 1 - 2 * column)
    partner = at_xy(cy, 3 - cx)
    crossed = (cy * SIDE + 3 - cx, cz * 2 + 1 - core)

    def at_z(z):
        return (ctx, mod(z) * 2 + core)

    barrier = pltpu.get_barrier_semaphore()
    others = [at_xy(cy, cx + d) for d in (1, 2, 3)] + [at_xy(cy + d, cx) for d in (1, 2, 3)]
    others += [at_z(cz + 1), at_z(cz - 1), sibling, following, previous, crossed]
    for other in others:
        pl.semaphore_signal(barrier, inc=1, device_id=other, device_id_type=MESH)

    sources = (q_hbm, k_hbm, v_hbm)

    def own_copy(n):
        return pltpu.make_async_copy(
            w_ref.at[:, pl.ds(n * CHUNK, CHUNK)], wbuf.at[n, cy * 2 + column], own_sem.at[n])

    def in_copy(index):
        return pltpu.make_async_copy(sources[index], inputs.at[index], in_sem.at[index])

    for n in range(CHUNKS):
        own_copy(n).start()
    for index in (1, 2, 0):
        in_copy(index).start()
    for n in range(CHUNKS):
        own_copy(n).wait()
    pl.semaphore_wait(barrier, len(others))

    def halo_copy(index):
        return pltpu.make_async_remote_copy(
            src_ref=sources[index].at[pl.ds(ROWS - HALO, HALO)], dst_ref=halo.at[index],
            send_sem=h_send.at[index], recv_sem=h_recv.at[index],
            device_id=following, device_id_type=MESH)

    for index in (1, 2, 0):
        halo_copy(index).start()

    def ring(kind, receiving):
        step = 1 if kind % 2 == 0 else -1
        if receiving:
            return step, (-step if kind < 2 else -2 * step)
        return step, (0 if kind < 2 else -step)

    def w_copy(n, number, receiving):
        if number < 4 or number >= 9:
            kind = number if number < 4 else (number - 9) % 4
            step, back = ring(kind, receiving)
            row = cy + back
            flip = number >= 13
            target = at_xy(cy + step, cx)
            low, high = (0, CUT) if number < 4 else (CUT, ROWS)
            middle = (low + high) // 2
            if kind == 2:
                high = middle
            if kind == 3:
                low = middle
        else:
            row = cy + (OFFS[number - 4] if number < 8 else 0)
            flip = receiving
            target = beside
            low, high = (0, CUT) if number < 8 else (CUT, ROWS)
        across = 1 - column if flip else column
        where = wbuf.at[n, mod(row) * 2 + across, pl.ds(low, high - low)]
        index = n * PER_CHUNK + number
        return pltpu.make_async_remote_copy(
            src_ref=where, dst_ref=where, send_sem=w_send.at[index], recv_sem=w_recv.at[index],
            device_id=target, device_id_type=MESH)

    def w_start(n, *numbers):
        for number in numbers:
            w_copy(n, number, False).start()

    def w_wait(n, *numbers):
        for number in numbers:
            w_copy(n, number, True).wait_recv()

    def w_own(n):
        w_start(n, 8, 0, 1, 9, 10, 4)

    def w_first(n):
        w_wait(n, 8)
        w_start(n, 13, 14)
        for kind in (0, 1):
            w_wait(n, kind)
            w_start(n, kind + 2, 5 + kind)
        for kind in (0, 1):
            w_wait(n, 9 + kind)
            w_start(n, 11 + kind)

    def w_second(n):
        w_wait(n, 2, 3)
        w_start(n, 7)
        for kind in (0, 1):
            w_wait(n, 13 + kind)
            w_start(n, 15 + kind)

    def w_third(n):
        w_wait(n, 4, 5, 6, 7, 11, 12, 15, 16)

    def a_copy(q, kind, receiving):
        low, size = 0, ROWS
        held = role
        if kind < 4:
            step, back = ring(kind, receiving)
            if kind >= 2:
                low, size = (ROWS // 2 if kind == 3 else 0), ROWS // 2
            target = at_z(cz + step)
        else:
            back = OFFS[kind - 4]
            held = 1 - role if receiving else role
            target = sibling
        where = abuf.at[held * SIDE + mod(cz + back), q, pl.ds(low, size)]
        index = q * 8 + kind
        return pltpu.make_async_remote_copy(
            src_ref=where, dst_ref=where, send_sem=a_send.at[index], recv_sem=a_recv.at[index],
            device_id=target, device_id_type=MESH)

    def p_copy(q):
        return pltpu.make_async_remote_copy(
            src_ref=abuf.at[2 * SIDE, q], dst_ref=abuf.at[SIDE + cz, q],
            send_sem=p_send.at[q], recv_sem=p_recv.at[q],
            device_id=crossed, device_id_type=MESH)

    def c_copy(n):
        return pltpu.make_async_remote_copy(
            src_ref=cout.at[n], dst_ref=cin.at[n], send_sem=c_send.at[n], recv_sem=c_recv.at[n],
            device_id=partner, device_id_type=MESH)

    def state_copy(part, stage, distance, receiving):
        held = (xstate, ystate)[stage]
        position = (cx, cy)[stage]
        index = mod(position - distance) if receiving else position
        target = at_xy(cy, cx + distance) if stage == 0 else at_xy(cy + distance, cx)
        number = part * 6 + stage * 3 + distance - 1
        where = held.at[part, index]
        return pltpu.make_async_remote_copy(
            src_ref=where, dst_ref=where,
            send_sem=s_send.at[number], recv_sem=s_recv.at[number],
            device_id=target, device_id_type=MESH)

    w_own(0)
    w_own(1)

    dec[...] = jnp.exp(-rates_ref[...])

    def lanes_of(tile):
        return pl.ds(pl.multiple_of(tile * LANES, LANES), LANES)

    def widen(index):
        in_copy(index).wait()

        def body(tile, carry):
            streams[index, tile, pl.ds(0, PAD), :] = jnp.zeros((PAD, LANES), F32)
            streams[index, tile, pl.ds(PAD, ROWS), :] = inputs[index, :, lanes_of(tile)].astype(F32)
            return carry

        lax.fori_loop(0, TILES, body, 0)

    def widen_halo(index):
        halo_copy(index).wait_recv()
        keep = jnp.where(ctx > 0, 1.0, 0.0).astype(F32)

        def body(tile, carry):
            rim = halo[index, :, lanes_of(tile)].astype(F32)
            streams[index, tile, pl.ds(0, PAD), :] = rim[HALO - PAD:] * keep
            return carry

        lax.fori_loop(0, TILES, body, 0)

    def spread(row):
        return jnp.broadcast_to(row, (SEGS, LANES))

    def strided(index, tile, start):
        return streams[index, tile, pl.ds(start, SEGS, stride=STEPS), :]

    def tap_rows(index, lanes):
        return [spread(taps_ref[index, pl.ds(j, 1), lanes]) for j in range(3)]

    def gate(k_taps, v_taps, k0, k1, k2, v0, v1, v2):
        kf = rounded(k_taps[0] * k0 + k_taps[1] * k1 + k_taps[2] * k2)
        vf = rounded(v_taps[0] * v0 + v_taps[1] * v1 + v_taps[2] * v2)
        return rounded(kf * vf)

    def first_tile(tile, carry):
        lanes = lanes_of(tile)
        decay = [spread(dec[pl.ds(r, 1), lanes]) for r in range(ORDER)]
        k_taps, v_taps = tap_rows(1, lanes), tap_rows(2, lanes)

        def step(i, held):
            k1, k2, v1, v2, states = held
            k0, v0 = strided(1, tile, PAD + i), strided(2, tile, PAD + i)
            gated = gate(k_taps, v_taps, k0, k1, k2, v0, v1, v2)
            gbuf[tile, i] = gated
            states = tuple(decay[r] * states[r] + gated for r in range(ORDER))
            return k0, k1, v0, v1, states

        zero = jnp.zeros((SEGS, LANES), F32)
        start = (strided(1, tile, PAD - 1), strided(1, tile, PAD - 2),
                 strided(2, tile, PAD - 1), strided(2, tile, PAD - 2), (zero,) * ORDER)
        states = lax.fori_loop(0, STEPS, step, start, unroll=4)[4]
        for r in range(ORDER):
            ends[tile, pl.ds(r, SEGS, stride=ORDER), :] = states[r]
        return carry

    def mend_tile(tile, carry):
        lanes = lanes_of(tile)
        k_taps, v_taps = tap_rows(1, lanes), tap_rows(2, lanes)
        k = [strided(1, tile, PAD + d) for d in (-2, -1, 0, 1)]
        v = [strided(2, tile, PAD + d) for d in (-2, -1, 0, 1)]
        changes = []
        for i in (0, 1):
            gated = gate(k_taps, v_taps, k[i + 2], k[i + 1], k[i], v[i + 2], v[i + 1], v[i])
            changes.append(gated - gbuf[tile, i])
            gbuf[tile, i] = gated
        rate = rates_ref[:, lanes]
        far, near = jnp.exp(-float(STEPS - 1) * rate), jnp.exp(-float(STEPS - 2) * rate)
        for r in range(ORDER):
            rows = pl.ds(r, SEGS, stride=ORDER)
            ends[tile, rows, :] = (ends[tile, rows, :] + spread(far[r:r + 1]) * changes[0]
                                   + spread(near[r:r + 1]) * changes[1])
        return carry

    def combine_tile(part):
        def body(tile, carry):
            jump = jnp.exp(-float(STEPS) * rates_ref[:, lanes_of(tile)])
            state = jnp.zeros((ORDER, LANES), F32)
            for seg in range(SEGS):
                inits[tile, pl.ds(seg * ORDER, ORDER), :] = state
                state = jump * state + ends[tile, pl.ds(seg * ORDER, ORDER), :]
            xstate[part, cx, :, lanes_of(tile - part * (TILES // PARTS))] = state
            return carry
        return body

    def row_tile(part):
        def body(tile, carry):
            lanes = lanes_of(tile - part * (TILES // PARTS))
            jump = jnp.exp(-float(ROWS) * rates_ref[:, lanes_of(tile)])
            state = jnp.zeros((ORDER, LANES), F32)
            for position in range(SIDE):
                state = jump * state + xstate[part, position, :, lanes]
            ystate[part, cy, :, lanes] = state
            return carry
        return body

    def seed_tile(part):
        def body(tile, carry):
            lanes = lanes_of(tile - part * (TILES // PARTS))
            rate = rates_ref[:, lanes_of(tile)]
            jump_x = jnp.exp(-float(ROWS) * rate)
            jump_y = jnp.exp(-float(ROWS * SIDE) * rate)
            before_x = jnp.zeros((ORDER, LANES), F32)
            before_y = jnp.zeros((ORDER, LANES), F32)
            for position in range(SIDE - 1):
                before_x = jnp.where(
                    position < cx, jump_x * before_x + xstate[part, position, :, lanes], before_x)
                before_y = jnp.where(
                    position < cy, jump_y * before_y + ystate[part, position, :, lanes], before_y)
            shift = (cx * ROWS).astype(F32)
            state = before_x + jnp.exp(-shift * rate) * before_y
            jump = jnp.exp(-float(STEPS) * rate)
            for seg in range(SEGS):
                rows = pl.ds(seg * ORDER, ORDER)
                inits[tile, rows, :] = inits[tile, rows, :] + state
                state = jump * state
            return carry
        return body

    target_block = jnp.where(role == 0, cz, 2 * SIDE)

    def second_tile(part):
        def body(tile, carry):
            lanes = lanes_of(tile)
            decay = [spread(dec[pl.ds(r, 1), lanes]) for r in range(ORDER)]
            weight = [spread(res_ref[pl.ds(r, 1), lanes]) for r in range(ORDER)]
            q_taps = tap_rows(0, lanes)

            def step(i, held):
                q1, q2, states = held
                q0 = strided(0, tile, PAD + i)
                qf = rounded(q_taps[0] * q0 + q_taps[1] * q1 + q_taps[2] * q2)
                gated = gbuf[tile, i]
                states = tuple(decay[r] * states[r] + gated for r in range(ORDER))
                terms = [weight[r] * states[r] for r in range(ORDER)]
                while len(terms) > 1:
                    terms = [terms[j] + terms[j + 1] for j in range(0, len(terms), 2)]
                ybuf[pl.ds(i, SEGS, stride=STEPS), :] = qf * terms[0]
                return q0, q1, states

            start = (strided(0, tile, PAD - 1), strided(0, tile, PAD - 2),
                     tuple(inits[tile, pl.ds(r, SEGS, stride=ORDER), :] for r in range(ORDER)))
            lax.fori_loop(0, STEPS, step, start, unroll=4)
            abuf[target_block, part, :, lanes_of(tile - part * (TILES // PARTS))] = (
                ybuf[...].astype(BF16))
            return carry
        return body

    def tiles(part, body):
        each = TILES // PARTS
        lax.fori_loop(part * each, (part + 1) * each, body, 0)

    def states_out(part, stage):
        for distance in (1, 3, 2):
            state_copy(part, stage, distance, False).start()

    def states_in(part, stage):
        for distance in (1, 3, 2):
            state_copy(part, stage, distance, True).wait_recv()

    def a_begin(q):
        @pl.when(role == 0)
        def _():
            for kind in (0, 1, 4):
                a_copy(q, kind, False).start()

        @pl.when(role == 1)
        def _():
            p_copy(q).start()

    def a_cross(q):
        @pl.when(role == 1)
        def _():
            p_copy(q).wait_recv()
            for kind in (0, 1, 4):
                a_copy(q, kind, False).start()

    def a_middle(q):
        for kind in (0, 1):
            a_copy(q, kind, True).wait_recv()
            a_copy(q, kind + 2, False).start()
            a_copy(q, kind + 5, False).start()

    def a_end(q):
        for kind in (2, 3):
            a_copy(q, kind, True).wait_recv()
        a_copy(q, 7, False).start()

    def a_sibling(q, *kinds):
        for kind in kinds:
            a_copy(q, kind, True).wait_recv()

    def multiply(group, z, q, n):
        block = mod(z)
        acc[group, n] += jnp.dot(
            abuf[group * SIDE + block, q], wbuf[n, block * 2 + q], preferred_element_type=F32)

    def sweep(groups, offsets, parts, chunks):
        g0, gn = groups
        o0, on = offsets
        q0, qn = parts
        n0, nn = chunks

        def body(t, carry):
            n = n0 + t // (gn * on * qn)
            rest = t % (gn * on * qn)
            multiply(g0 + rest // (on * qn), cz + o0 + rest % on, q0 + (rest // on) % qn, n)
            return carry

        lax.fori_loop(0, gn * on * qn * nn, body, 0)

    def c_begin(n):
        cout[n] = acc[1, n].astype(BF16)
        c_copy(n).start()

    def c_end(n):
        c_copy(n).wait_recv()
        out_ref[:, pl.ds(n * CHUNK, CHUNK)] = (acc[0, n] + cin[n].astype(F32)).astype(BF16)

    NEAR, FAR, EVERY = (-1, 3), (2, 1), (-1, 4)
    BOTH, OWN, THEIRS = (0, 2), (0, 1), (1, 1)

    widen(1)
    widen(2)
    tiles(0, first_tile)
    widen_halo(1)
    widen_halo(2)
    tiles(0, mend_tile)
    tiles(0, combine_tile(0))
    states_out(0, 0)
    tiles(1, first_tile)
    tiles(1, mend_tile)
    tiles(1, combine_tile(1))
    states_out(1, 0)
    w_first(0)
    w_own(2)
    states_in(0, 0)
    tiles(0, row_tile(0))
    states_out(0, 1)
    widen(0)
    widen_halo(0)
    states_in(1, 0)
    tiles(1, row_tile(1))
    states_out(1, 1)
    w_second(0)
    states_in(0, 1)
    tiles(0, seed_tile(0))
    tiles(0, second_tile(0))
    a_begin(0)
    w_first(1)
    w_own(3)
    states_in(1, 1)
    tiles(1, seed_tile(1))
    tiles(1, second_tile(1))
    a_begin(1)
    w_second(1)
    w_third(0)
    acc[...] = jnp.zeros_like(acc)
    a_cross(0)
    w_first(2)
    a_cross(1)
    a_middle(0)
    w_second(2)
    w_third(1)
    a_middle(1)
    w_first(3)
    a_end(0)
    a_sibling(0, 4, 5, 6)
    sweep(BOTH, NEAR, (0, 1), (0, 2))
    w_third(2)
    w_second(3)
    a_end(1)
    a_sibling(1, 4, 5, 6)
    sweep(BOTH, NEAR, (1, 1), (0, 2))
    a_sibling(0, 7)
    a_sibling(1, 7)
    sweep(THEIRS, FAR, (0, 2), (0, 1))
    c_begin(0)
    sweep(THEIRS, FAR, (0, 2), (1, 1))
    c_begin(1)
    sweep(THEIRS, EVERY, (0, 2), (2, 1))
    c_begin(2)
    sweep(OWN, FAR, (0, 2), (0, 2))
    sweep(OWN, EVERY, (0, 2), (2, 1))
    w_third(3)
    sweep(THEIRS, EVERY, (0, 2), (3, 1))
    c_begin(3)
    sweep(OWN, EVERY, (0, 2), (3, 1))
    for n in range(CHUNKS):
        c_end(n)

    for n in range(CHUNKS):
        for number in range(PER_CHUNK):
            w_copy(n, number, False).wait_send()
        c_copy(n).wait_send()
    for q in range(PARTS):
        for kind in range(8):
            a_copy(q, kind, False).wait_send()
        for stage in range(2):
            for distance in (1, 2, 3):
                state_copy(q, stage, distance, False).wait_send()

    @pl.when(role == 1)
    def _():
        for q in range(PARTS):
            p_copy(q).wait_send()

    for index in range(3):
        halo_copy(index).wait_send()


def per_device(query, keys_in, values_in, short_taps, mode_rates, mode_residues, out_weight):
    vmem = pl.BlockSpec(memory_space=pltpu.VMEM)
    hbm = pl.BlockSpec(memory_space=pl.ANY)
    dma = pltpu.SemaphoreType.DMA
    return pl.pallas_call(
        kernel,
        out_shape=jax.ShapeDtypeStruct((ROWS, WIDTH), BF16),
        in_specs=[hbm] * 3 + [vmem] * 3 + [hbm],
        out_specs=vmem,
        scratch_shapes=[
            pltpu.VMEM((CHUNKS, 2 * SIDE, ROWS, CHUNK), BF16),
            pltpu.VMEM((2 * SIDE + 1, PARTS, ROWS, PART), BF16),
            pltpu.VMEM((2, CHUNKS, ROWS, CHUNK), F32),
            pltpu.VMEM((CHUNKS, ROWS, CHUNK), BF16),
            pltpu.VMEM((CHUNKS, ROWS, CHUNK), BF16),
            pltpu.VMEM((3, ROWS, WIDTH), BF16),
            pltpu.VMEM((3, TILES, PAD + ROWS, LANES), F32),
            pltpu.VMEM((TILES, STEPS, SEGS, LANES), F32),
            pltpu.VMEM((ROWS, LANES), F32),
            pltpu.VMEM((3, HALO, WIDTH), BF16),
            pltpu.VMEM((ORDER, WIDTH), F32),
            pltpu.VMEM((TILES, SEGS * ORDER, LANES), F32),
            pltpu.VMEM((TILES, SEGS * ORDER, LANES), F32),
            pltpu.VMEM((PARTS, SIDE, ORDER, PART), F32),
            pltpu.VMEM((PARTS, SIDE, ORDER, PART), F32),
            dma((CHUNKS * PER_CHUNK,)), dma((CHUNKS * PER_CHUNK,)),
            dma((PARTS * 8,)), dma((PARTS * 8,)), dma((PARTS,)), dma((PARTS,)),
            dma((CHUNKS,)), dma((CHUNKS,)), dma((3,)), dma((3,)),
            dma((PARTS * 6,)), dma((PARTS * 6,)), dma((CHUNKS,)), dma((3,)),
        ],
        compiler_params=pltpu.CompilerParams(
            collective_id=0, has_side_effects=True, vmem_limit_bytes=56 * 1024 * 1024),
        cost_estimate=pl.CostEstimate(
            flops=2 * ROWS * 8192 * WIDTH, bytes_accessed=6 * 1024 * 1024, transcendentals=0),
    )(query, keys_in, values_in, short_taps, mode_rates, mode_residues, out_weight)


def solution(mesh):
    in_specs = (
        P("ctx", "ch"),
        P("ctx", "ch"),
        P("ctx", "ch"),
        P(None, None, "ch"),
        P(None, "ch"),
        P(None, "ch"),
        P("ctx", "ch"),
    )
    return jax.shard_map(
        per_device, mesh=mesh, in_specs=in_specs, out_specs=P("ctx", "ch"), check_vma=False
    )
```

```python
import jax
import jax.numpy as jnp
from jax import lax
from jax.experimental import pallas as pl
from jax.experimental.pallas import tpu as pltpu
from jax.sharding import PartitionSpec as P

MESH = pl.DeviceIdType.MESH
SIDE = 4
ORDER = 16
ROWS = 512
WIDTH = 1024
LANES = 128
TILES = WIDTH // LANES
SEGS = 8
STEPS = ROWS // SEGS
PAD = 8
HALO = 16
PARTS = 2
PART = WIDTH // PARTS
PIECES = 4
PIECE = WIDTH // PIECES
CHUNKS = 4
CHUNK = WIDTH // CHUNKS
CUT = 224
OFFS = (0, -1, 1, 2)
PER_GROUP = 17
GROUPS = ((0, 1), (1, 2), (3, 1))
F32 = jnp.float32
BF16 = jnp.bfloat16


def kernel(
    q_hbm, k_hbm, v_hbm, taps_ref, rates_ref, res_ref, w_ref, out_ref,
    wbuf, abuf, acc, cout, cin, inputs, streams, gbuf, ybuf, halo, dec, ends, inits, xstate, ystate,
    w_send, w_recv, a_send, a_recv, p_send, p_recv, c_send, c_recv, h_send, h_recv, s_send, s_recv,
    own_sem, in_sem,
):
    ctx = lax.axis_index("ctx")
    ch = lax.axis_index("ch")
    cy, cx = ctx // SIDE, ctx % SIDE
    cz, core = ch // 2, ch % 2
    column, side = cx % 2, cx // 2
    role = jnp.where(core == side, 0, 1)

    def mod(value):
        return lax.rem(value + 2 * SIDE, SIDE)

    def at_xy(y, x):
        return (mod(y) * SIDE + mod(x), ch)

    following = (lax.rem(ctx + 1, SIDE * SIDE), ch)
    previous = (lax.rem(ctx + SIDE * SIDE - 1, SIDE * SIDE), ch)
    sibling = (ctx, cz * 2 + 1 - core)
    beside = at_xy(cy, cx + 1 - 2 * column)
    partner = at_xy(cy, 3 - cx)
    crossed = (cy * SIDE + 3 - cx, cz * 2 + 1 - core)

    def at_z(z):
        return (ctx, mod(z) * 2 + core)

    barrier = pltpu.get_barrier_semaphore()
    others = [at_xy(cy, cx + d) for d in (1, 2, 3)] + [at_xy(cy + d, cx) for d in (1, 2, 3)]
    others += [at_z(cz + 1), at_z(cz - 1), sibling, following, previous, crossed]
    for other in others:
        pl.semaphore_signal(barrier, inc=1, device_id=other, device_id_type=MESH)

    sources = (q_hbm, k_hbm, v_hbm)

    def own_copy(n):
        return pltpu.make_async_copy(
            w_ref.at[:, pl.ds(n * CHUNK, CHUNK)], wbuf.at[cy * 2 + column, n], own_sem.at[n])

    def in_copy(index):
        return pltpu.make_async_copy(sources[index], inputs.at[index], in_sem.at[index])

    for n in range(CHUNKS):
        own_copy(n).start()
    for index in (1, 2, 0):
        in_copy(index).start()
    def halo_copy(index):
        return pltpu.make_async_remote_copy(
            src_ref=sources[index].at[pl.ds(ROWS - HALO, HALO)], dst_ref=halo.at[index],
            send_sem=h_send.at[index], recv_sem=h_recv.at[index],
            device_id=following, device_id_type=MESH)

    def enter():
        pl.semaphore_wait(barrier, len(others))
        for index in (1, 2, 0):
            halo_copy(index).start()
        for n in range(CHUNKS):
            own_copy(n).wait()

    def ring(kind, receiving):
        step = 1 if kind % 2 == 0 else -1
        if receiving:
            return step, (-step if kind < 2 else -2 * step)
        return step, (0 if kind < 2 else -step)

    def w_copy(n, number, receiving):
        if number < 4 or number >= 9:
            kind = number if number < 4 else (number - 9) % 4
            step, back = ring(kind, receiving)
            row = cy + back
            flip = number >= 13
            target = at_xy(cy + step, cx)
            low, high = (0, CUT) if number < 4 else (CUT, ROWS)
            middle = (low + high) // 2
            if kind == 2:
                high = middle
            if kind == 3:
                low = middle
        else:
            row = cy + (OFFS[number - 4] if number < 8 else 0)
            flip = receiving
            target = beside
            low, high = (0, CUT) if number < 8 else (CUT, ROWS)
        across = 1 - column if flip else column
        where = wbuf.at[mod(row) * 2 + across, pl.ds(*GROUPS[n]), pl.ds(low, high - low)]
        index = n * PER_GROUP + number
        return pltpu.make_async_remote_copy(
            src_ref=where, dst_ref=where, send_sem=w_send.at[index], recv_sem=w_recv.at[index],
            device_id=target, device_id_type=MESH)

    def w_start(n, *numbers):
        for number in numbers:
            w_copy(n, number, False).start()

    def w_wait(n, *numbers):
        for number in numbers:
            w_copy(n, number, True).wait_recv()

    def w_own(n):
        w_start(n, 8, 0, 1, 9, 10, 4)

    def w_first(n):
        w_wait(n, 8)
        w_start(n, 13, 14)
        for kind in (0, 1):
            w_wait(n, kind)
            w_start(n, kind + 2, 5 + kind)
        for kind in (0, 1):
            w_wait(n, 9 + kind)
            w_start(n, 11 + kind)

    def w_second(n):
        w_wait(n, 2, 3)
        w_start(n, 7)
        for kind in (0, 1):
            w_wait(n, 13 + kind)
            w_start(n, 15 + kind)

    def w_third(n):
        w_wait(n, 4, 5, 6, 7, 11, 12, 15, 16)

    def a_copy(q, kind, receiving):
        low, size = 0, ROWS
        held = role
        if kind < 4:
            step, back = ring(kind, receiving)
            if kind >= 2:
                low, size = (ROWS // 2 if kind == 3 else 0), ROWS // 2
            target = at_z(cz + step)
        else:
            back = OFFS[kind - 4]
            held = 1 - role if receiving else role
            target = sibling
        where = abuf.at[held * SIDE + mod(cz + back), q, pl.ds(low, size)]
        index = q * 8 + kind
        return pltpu.make_async_remote_copy(
            src_ref=where, dst_ref=where, send_sem=a_send.at[index], recv_sem=a_recv.at[index],
            device_id=target, device_id_type=MESH)

    def p_copy(q):
        return pltpu.make_async_remote_copy(
            src_ref=abuf.at[2 * SIDE, q], dst_ref=abuf.at[SIDE + cz, q],
            send_sem=p_send.at[q], recv_sem=p_recv.at[q],
            device_id=crossed, device_id_type=MESH)

    def c_copy(n):
        return pltpu.make_async_remote_copy(
            src_ref=cout.at[n], dst_ref=cin.at[n], send_sem=c_send.at[n], recv_sem=c_recv.at[n],
            device_id=partner, device_id_type=MESH)

    def state_copy(part, stage, distance, receiving):
        held = (xstate, ystate)[stage]
        position = (cx, cy)[stage]
        index = mod(position - distance) if receiving else position
        target = at_xy(cy, cx + distance) if stage == 0 else at_xy(cy + distance, cx)
        number = part * 6 + stage * 3 + distance - 1
        where = held.at[part, index]
        return pltpu.make_async_remote_copy(
            src_ref=where, dst_ref=where,
            send_sem=s_send.at[number], recv_sem=s_recv.at[number],
            device_id=target, device_id_type=MESH)


    dec[...] = jnp.exp(-rates_ref[...])

    def lanes_of(tile):
        return pl.ds(pl.multiple_of(tile * LANES, LANES), LANES)

    def widen(index):
        in_copy(index).wait()

        def body(tile, carry):
            streams[index, tile, pl.ds(0, PAD), :] = jnp.zeros((PAD, LANES), F32)
            streams[index, tile, pl.ds(PAD, ROWS), :] = inputs[index, :, lanes_of(tile)].astype(F32)
            return carry

        lax.fori_loop(0, TILES, body, 0)

    def widen_halo(index):
        halo_copy(index).wait_recv()
        keep = jnp.where(ctx > 0, 1.0, 0.0).astype(F32)

        def body(tile, carry):
            rim = halo[index, :, lanes_of(tile)].astype(F32)
            streams[index, tile, pl.ds(0, PAD), :] = rim[HALO - PAD:] * keep
            return carry

        lax.fori_loop(0, TILES, body, 0)

    def spread(row):
        return jnp.broadcast_to(row, (SEGS, LANES))

    def strided(index, tile, start):
        return streams[index, tile, pl.ds(start, SEGS, stride=STEPS), :]

    def tap_rows(index, lanes):
        return [spread(taps_ref[index, pl.ds(j, 1), lanes]) for j in range(3)]

    def gate(k_taps, v_taps, k0, k1, k2, v0, v1, v2):
        kf = k_taps[0] * k0 + k_taps[1] * k1 + k_taps[2] * k2
        vf = v_taps[0] * v0 + v_taps[1] * v1 + v_taps[2] * v2
        return kf * vf

    def first_tile(tile, carry):
        lanes = lanes_of(tile)
        decay = [spread(dec[pl.ds(r, 1), lanes]) for r in range(ORDER)]
        k_taps, v_taps = tap_rows(1, lanes), tap_rows(2, lanes)

        def step(i, held):
            k1, k2, v1, v2, states = held
            k0, v0 = strided(1, tile, PAD + i), strided(2, tile, PAD + i)
            gated = gate(k_taps, v_taps, k0, k1, k2, v0, v1, v2)
            gbuf[tile, i] = gated
            states = tuple(decay[r] * states[r] + gated for r in range(ORDER))
            return k0, k1, v0, v1, states

        zero = jnp.zeros((SEGS, LANES), F32)
        start = (strided(1, tile, PAD - 1), strided(1, tile, PAD - 2),
                 strided(2, tile, PAD - 1), strided(2, tile, PAD - 2), (zero,) * ORDER)
        states = lax.fori_loop(0, STEPS, step, start, unroll=4)[4]
        for r in range(ORDER):
            ends[tile, pl.ds(r, SEGS, stride=ORDER), :] = states[r]
        return carry

    def mend_tile(tile, carry):
        lanes = lanes_of(tile)
        k_taps, v_taps = tap_rows(1, lanes), tap_rows(2, lanes)
        k = [strided(1, tile, PAD + d) for d in (-2, -1, 0, 1)]
        v = [strided(2, tile, PAD + d) for d in (-2, -1, 0, 1)]
        changes = []
        for i in (0, 1):
            gated = gate(k_taps, v_taps, k[i + 2], k[i + 1], k[i], v[i + 2], v[i + 1], v[i])
            changes.append(gated - gbuf[tile, i])
            gbuf[tile, i] = gated
        rate = rates_ref[:, lanes]
        far, near = jnp.exp(-float(STEPS - 1) * rate), jnp.exp(-float(STEPS - 2) * rate)
        for r in range(ORDER):
            rows = pl.ds(r, SEGS, stride=ORDER)
            ends[tile, rows, :] = (ends[tile, rows, :] + spread(far[r:r + 1]) * changes[0]
                                   + spread(near[r:r + 1]) * changes[1])
        return carry

    def combine_tile(part):
        def body(tile, carry):
            jump = jnp.exp(-float(STEPS) * rates_ref[:, lanes_of(tile)])
            state = jnp.zeros((ORDER, LANES), F32)
            for seg in range(SEGS):
                inits[tile, pl.ds(seg * ORDER, ORDER), :] = state
                state = jump * state + ends[tile, pl.ds(seg * ORDER, ORDER), :]
            xstate[part, cx, :, lanes_of(tile - part * (TILES // PARTS))] = state
            return carry
        return body

    def row_tile(part):
        def body(tile, carry):
            lanes = lanes_of(tile - part * (TILES // PARTS))
            jump = jnp.exp(-float(ROWS) * rates_ref[:, lanes_of(tile)])
            state = jnp.zeros((ORDER, LANES), F32)
            for position in range(SIDE):
                state = jump * state + xstate[part, position, :, lanes]
            ystate[part, cy, :, lanes] = state
            return carry
        return body

    def seed_tile(part):
        def body(tile, carry):
            lanes = lanes_of(tile - part * (TILES // PARTS))
            rate = rates_ref[:, lanes_of(tile)]
            jump_x = jnp.exp(-float(ROWS) * rate)
            jump_y = jnp.exp(-float(ROWS * SIDE) * rate)
            before_x = jnp.zeros((ORDER, LANES), F32)
            before_y = jnp.zeros((ORDER, LANES), F32)
            for position in range(SIDE - 1):
                before_x = jnp.where(
                    position < cx, jump_x * before_x + xstate[part, position, :, lanes], before_x)
                before_y = jnp.where(
                    position < cy, jump_y * before_y + ystate[part, position, :, lanes], before_y)
            shift = (cx * ROWS).astype(F32)
            state = before_x + jnp.exp(-shift * rate) * before_y
            jump = jnp.exp(-float(STEPS) * rate)
            for seg in range(SEGS):
                rows = pl.ds(seg * ORDER, ORDER)
                inits[tile, rows, :] = inits[tile, rows, :] + state
                state = jump * state
            return carry
        return body

    target_block = jnp.where(role == 0, cz, 2 * SIDE)

    def second_tile(tile, carry):
        lanes = lanes_of(tile)
        decay = [spread(dec[pl.ds(r, 1), lanes]) for r in range(ORDER)]
        weight = [spread(res_ref[pl.ds(r, 1), lanes]) for r in range(ORDER)]
        q_taps = tap_rows(0, lanes)

        def step(i, held):
            q1, q2, states = held
            q0 = strided(0, tile, PAD + i)
            qf = q_taps[0] * q0 + q_taps[1] * q1 + q_taps[2] * q2
            gated = gbuf[tile, i]
            states = tuple(decay[r] * states[r] + gated for r in range(ORDER))
            terms = [weight[r] * states[r] for r in range(ORDER)]
            while len(terms) > 1:
                terms = [terms[j] + terms[j + 1] for j in range(0, len(terms), 2)]
            ybuf[pl.ds(i, SEGS, stride=STEPS), :] = qf * terms[0]
            return q0, q1, states

        start = (strided(0, tile, PAD - 1), strided(0, tile, PAD - 2),
                 tuple(inits[tile, pl.ds(r, SEGS, stride=ORDER), :] for r in range(ORDER)))
        lax.fori_loop(0, STEPS, step, start, unroll=4)
        abuf[target_block, tile // 2, :, lanes_of(tile % 2)] = ybuf[...].astype(BF16)
        return carry

    def tiles(part, body):
        each = TILES // PARTS
        lax.fori_loop(part * each, (part + 1) * each, body, 0)

    def outputs(q):
        lax.fori_loop(2 * q, 2 * q + 2, second_tile, 0)

    def states_out(part, stage):
        for distance in (1, 3, 2):
            state_copy(part, stage, distance, False).start()

    def states_in(part, stage):
        for distance in (1, 3, 2):
            state_copy(part, stage, distance, True).wait_recv()

    def when(wanted, call, *args):
        @pl.when(role == wanted)
        def _():
            call(*args)

    def a_start(q, *kinds):
        for kind in kinds:
            a_copy(q, kind, False).start()

    def p_begin(q):
        p_copy(q).start()

    def a_cross(q):
        p_copy(q).wait_recv()
        a_start(q, 0, 1, 4)

    def a_middle(q):
        for kind in (0, 1):
            a_copy(q, kind, True).wait_recv()
            a_copy(q, kind + 2, False).start()
            a_copy(q, kind + 5, False).start()

    def a_end(q):
        for kind in (2, 3):
            a_copy(q, kind, True).wait_recv()
        a_copy(q, 7, False).start()

    def a_sibling(q, *kinds):
        for kind in kinds:
            a_copy(q, kind, True).wait_recv()

    def a_pair(q):
        a_sibling(q, 4, 5, 6, 7)

    def multiply(group, z, q, n):
        block = mod(z)
        total = acc[group, n]
        for s in range(2):
            total += jnp.dot(
                abuf[group * SIDE + block, 2 * q + s], wbuf[block * 2 + q, n, pl.ds(s * PIECE, PIECE)],
                preferred_element_type=F32)
        acc[group, n] = total

    def sweep(groups, offsets, parts, chunks):
        g0, gn = groups
        o0, on = offsets
        q0, qn = parts
        n0, nn = chunks

        def body(t, carry):
            n = n0 + t // (gn * on * qn)
            rest = t % (gn * on * qn)
            multiply(g0 + rest // (on * qn), cz + o0 + rest % on, q0 + (rest // on) % qn, n)
            return carry

        lax.fori_loop(0, gn * on * qn * nn, body, 0)

    def c_begin(n):
        cout[n] = acc[1, n].astype(BF16)
        c_copy(n).start()

    def c_end(n):
        c_copy(n).wait_recv()
        out_ref[:, pl.ds(n * CHUNK, CHUNK)] = (acc[0, n] + cin[n].astype(F32)).astype(BF16)

    NEAR, FAR, EVERY = (-1, 3), (2, 1), (-1, 4)
    BOTH, OWN, THEIRS = (0, 2), (0, 1), (1, 1)

    widen(1)
    widen(2)
    widen(0)
    enter()
    w_start(0, 8, 0, 1, 9, 10)
    tiles(0, first_tile)
    widen_halo(1)
    widen_halo(2)
    tiles(0, mend_tile)
    tiles(0, combine_tile(0))
    states_out(0, 0)
    tiles(1, first_tile)
    tiles(1, mend_tile)
    tiles(1, combine_tile(1))
    states_out(1, 0)
    widen_halo(0)
    states_in(0, 0)
    tiles(0, row_tile(0))
    states_out(0, 1)
    states_in(1, 0)
    tiles(1, row_tile(1))
    states_out(1, 1)
    w_start(0, 4)
    w_start(1, 8, 4)
    states_in(0, 1)
    tiles(0, seed_tile(0))
    outputs(0)
    when(1, p_begin, 0)
    when(0, a_start, 0, 0, 1, 4)
    outputs(1)
    when(1, p_begin, 1)
    when(0, a_start, 1, 0, 1, 4)
    states_in(1, 1)
    w_first(0)
    w_start(1, 0, 1, 9, 10)
    w_own(2)
    tiles(1, seed_tile(1))
    outputs(2)
    when(1, p_begin, 2)
    when(0, a_start, 2, 4)
    when(1, a_cross, 0)
    outputs(3)
    when(1, p_begin, 3)
    when(0, a_start, 3, 4)
    when(1, a_cross, 1)
    acc[...] = jnp.zeros_like(acc)
    when(1, a_middle, 0)
    w_second(0)
    when(1, a_cross, 2)
    when(1, a_middle, 1)
    when(1, a_cross, 3)
    when(1, a_end, 0)
    when(1, a_middle, 2)
    when(1, a_end, 1)
    when(1, a_middle, 3)
    when(0, a_middle, 0)
    when(0, a_middle, 1)
    when(0, a_start, 2, 0, 1)
    when(0, a_start, 3, 0, 1)
    w_first(1)
    when(1, a_end, 2)
    when(1, a_end, 3)
    w_third(0)
    when(0, a_pair, 0)
    when(0, a_pair, 1)
    sweep(THEIRS, EVERY, (0, 1), (0, 1))
    when(0, a_pair, 2)
    when(0, a_pair, 3)
    sweep(THEIRS, EVERY, (1, 1), (0, 1))
    c_begin(0)
    w_second(1)
    when(0, a_middle, 2)
    when(0, a_end, 0)
    when(0, a_middle, 3)
    when(0, a_end, 1)
    w_first(2)
    w_third(1)
    sweep(THEIRS, EVERY, (0, 2), (1, 1))
    c_begin(1)
    sweep(THEIRS, EVERY, (0, 2), (2, 1))
    c_begin(2)
    when(0, a_end, 2)
    when(0, a_end, 3)
    w_second(2)
    when(1, a_pair, 0)
    when(1, a_pair, 1)
    when(1, a_pair, 2)
    when(1, a_pair, 3)
    sweep(OWN, EVERY, (0, 2), (0, 3))
    w_third(2)
    sweep(THEIRS, EVERY, (0, 2), (3, 1))
    c_begin(3)
    sweep(OWN, EVERY, (0, 2), (3, 1))
    for n in range(CHUNKS):
        c_end(n)

    for n in range(len(GROUPS)):
        for number in range(PER_GROUP):
            w_copy(n, number, False).wait_send()
    for n in range(CHUNKS):
        c_copy(n).wait_send()
    for q in range(PIECES):
        for kind in range(8):
            a_copy(q, kind, False).wait_send()
    for q in range(PARTS):
        for stage in range(2):
            for distance in (1, 2, 3):
                state_copy(q, stage, distance, False).wait_send()

    @pl.when(role == 1)
    def _():
        for q in range(PIECES):
            p_copy(q).wait_send()

    for index in range(3):
        halo_copy(index).wait_send()


def per_device(query, keys_in, values_in, short_taps, mode_rates, mode_residues, out_weight):
    vmem = pl.BlockSpec(memory_space=pltpu.VMEM)
    hbm = pl.BlockSpec(memory_space=pl.ANY)
    dma = pltpu.SemaphoreType.DMA
    return pl.pallas_call(
        kernel,
        out_shape=jax.ShapeDtypeStruct((ROWS, WIDTH), BF16),
        in_specs=[hbm] * 3 + [vmem] * 3 + [hbm],
        out_specs=vmem,
        scratch_shapes=[
            pltpu.VMEM((2 * SIDE, CHUNKS, ROWS, CHUNK), BF16),
            pltpu.VMEM((2 * SIDE + 1, PIECES, ROWS, PIECE), BF16),
            pltpu.VMEM((2, CHUNKS, ROWS, CHUNK), F32),
            pltpu.VMEM((CHUNKS, ROWS, CHUNK), BF16),
            pltpu.VMEM((CHUNKS, ROWS, CHUNK), BF16),
            pltpu.VMEM((3, ROWS, WIDTH), BF16),
            pltpu.VMEM((3, TILES, PAD + ROWS, LANES), F32),
            pltpu.VMEM((TILES, STEPS, SEGS, LANES), F32),
            pltpu.VMEM((ROWS, LANES), F32),
            pltpu.VMEM((3, HALO, WIDTH), BF16),
            pltpu.VMEM((ORDER, WIDTH), F32),
            pltpu.VMEM((TILES, SEGS * ORDER, LANES), F32),
            pltpu.VMEM((TILES, SEGS * ORDER, LANES), F32),
            pltpu.VMEM((PARTS, SIDE, ORDER, PART), F32),
            pltpu.VMEM((PARTS, SIDE, ORDER, PART), F32),
            dma((len(GROUPS) * PER_GROUP,)), dma((len(GROUPS) * PER_GROUP,)),
            dma((PIECES * 8,)), dma((PIECES * 8,)), dma((PIECES,)), dma((PIECES,)),
            dma((CHUNKS,)), dma((CHUNKS,)), dma((3,)), dma((3,)),
            dma((PARTS * 6,)), dma((PARTS * 6,)), dma((CHUNKS,)), dma((3,)),
        ],
        compiler_params=pltpu.CompilerParams(
            collective_id=0, has_side_effects=True, vmem_limit_bytes=56 * 1024 * 1024),
        cost_estimate=pl.CostEstimate(
            flops=2 * ROWS * 8192 * WIDTH, bytes_accessed=6 * 1024 * 1024, transcendentals=0),
    )(query, keys_in, values_in, short_taps, mode_rates, mode_residues, out_weight)


def solution(mesh):
    in_specs = (
        P("ctx", "ch"),
        P("ctx", "ch"),
        P("ctx", "ch"),
        P(None, None, "ch"),
        P(None, "ch"),
        P(None, "ch"),
        P("ctx", "ch"),
    )
    return jax.shard_map(
        per_device, mesh=mesh, in_specs=in_specs, out_specs=P("ctx", "ch"), check_vma=False
    )
```

```python
import jax
import jax.numpy as jnp
from jax import lax
from jax.experimental import pallas as pl
from jax.experimental.pallas import tpu as pltpu
from jax.sharding import PartitionSpec as P

MESH = pl.DeviceIdType.MESH
SIDE = 4
ORDER = 16
ROWS = 512
WIDTH = 1024
LANES = 128
TILES = WIDTH // LANES
SEGS = 8
STEPS = ROWS // SEGS
PAD = 8
HALO = 16
PARTS = 2
PART = WIDTH // PARTS
PIECES = 4
PIECE = WIDTH // PIECES
CHUNKS = 4
CHUNK = WIDTH // CHUNKS
CUT = 224
OFFS = (0, -1, 1, 2)
PER_GROUP = 17
GROUPS = ((0, 2), (2, 1), (3, 1))
F32 = jnp.float32
BF16 = jnp.bfloat16


def kernel(
    q_hbm, k_hbm, v_hbm, taps_ref, rates_ref, res_ref, w_ref, out_ref,
    wbuf, abuf, acc, early, cout, cin, inputs, streams, gbuf, ybuf, halo, dec, ends, inits, xstate, ystate,
    w_send, w_recv, a_send, a_recv, p_send, p_recv, c_send, c_recv, h_send, h_recv, s_send, s_recv,
    own_sem, in_sem,
):
    ctx = lax.axis_index("ctx")
    ch = lax.axis_index("ch")
    cy, cx = ctx // SIDE, ctx % SIDE
    cz, core = ch // 2, ch % 2
    column, side = cx % 2, cx // 2
    role = jnp.where(core == side, 0, 1)

    def mod(value):
        return lax.rem(value + 2 * SIDE, SIDE)

    def at_xy(y, x):
        return (mod(y) * SIDE + mod(x), ch)

    following = (lax.rem(ctx + 1, SIDE * SIDE), ch)
    previous = (lax.rem(ctx + SIDE * SIDE - 1, SIDE * SIDE), ch)
    sibling = (ctx, cz * 2 + 1 - core)
    beside = at_xy(cy, cx + 1 - 2 * column)
    partner = at_xy(cy, 3 - cx)
    crossed = (cy * SIDE + 3 - cx, cz * 2 + 1 - core)

    def at_z(z):
        return (ctx, mod(z) * 2 + core)

    barrier = pltpu.get_barrier_semaphore()
    others = [at_xy(cy, cx + d) for d in (1, 2, 3)] + [at_xy(cy + d, cx) for d in (1, 2, 3)]
    others += [at_z(cz + 1), at_z(cz - 1), sibling, following, previous, crossed]
    for other in others:
        pl.semaphore_signal(barrier, inc=1, device_id=other, device_id_type=MESH)

    sources = (q_hbm, k_hbm, v_hbm)

    def own_copy(n):
        return pltpu.make_async_copy(
            w_ref.at[:, pl.ds(n * CHUNK, CHUNK)], wbuf.at[cy * 2 + column, n], own_sem.at[n])

    def in_copy(index):
        return pltpu.make_async_copy(sources[index], inputs.at[index], in_sem.at[index])

    for n in range(CHUNKS):
        own_copy(n).start()
    for index in (1, 2, 0):
        in_copy(index).start()
    def halo_copy(index):
        return pltpu.make_async_remote_copy(
            src_ref=sources[index].at[pl.ds(ROWS - HALO, HALO)], dst_ref=halo.at[index],
            send_sem=h_send.at[index], recv_sem=h_recv.at[index],
            device_id=following, device_id_type=MESH)

    def enter():
        pl.semaphore_wait(barrier, len(others))
        for index in (1, 2, 0):
            halo_copy(index).start()
        for n in range(CHUNKS):
            own_copy(n).wait()

    def ring(kind, receiving):
        step = 1 if kind % 2 == 0 else -1
        if receiving:
            return step, (-step if kind < 2 else -2 * step)
        return step, (0 if kind < 2 else -step)

    def w_copy(n, number, receiving):
        if number < 4 or number >= 9:
            kind = number if number < 4 else (number - 9) % 4
            step, back = ring(kind, receiving)
            row = cy + back
            flip = number >= 13
            target = at_xy(cy + step, cx)
            low, high = (0, CUT) if number < 4 else (CUT, ROWS)
            middle = (low + high) // 2
            if kind == 2:
                high = middle
            if kind == 3:
                low = middle
        else:
            row = cy + (OFFS[number - 4] if number < 8 else 0)
            flip = receiving
            target = beside
            low, high = (0, CUT) if number < 8 else (CUT, ROWS)
        across = 1 - column if flip else column
        where = wbuf.at[mod(row) * 2 + across, pl.ds(*GROUPS[n]), pl.ds(low, high - low)]
        index = n * PER_GROUP + number
        return pltpu.make_async_remote_copy(
            src_ref=where, dst_ref=where, send_sem=w_send.at[index], recv_sem=w_recv.at[index],
            device_id=target, device_id_type=MESH)

    def w_start(n, *numbers):
        for number in numbers:
            w_copy(n, number, False).start()

    def w_wait(n, *numbers):
        for number in numbers:
            w_copy(n, number, True).wait_recv()

    def w_own(n):
        w_start(n, 8, 0, 1, 9, 10, 4)

    def w_first(n):
        w_wait(n, 8)
        w_start(n, 13, 14)
        for kind in (0, 1):
            w_wait(n, kind)
            w_start(n, kind + 2, 5 + kind)
        for kind in (0, 1):
            w_wait(n, 9 + kind)
            w_start(n, 11 + kind)

    def w_second(n):
        w_wait(n, 2, 3)
        w_start(n, 7)
        for kind in (0, 1):
            w_wait(n, 13 + kind)
            w_start(n, 15 + kind)

    def w_third(n):
        w_wait(n, 4, 5, 6, 7, 11, 12, 15, 16)

    def a_copy(q, kind, receiving):
        low, size = 0, ROWS
        held = role
        if kind < 4:
            step, back = ring(kind, receiving)
            if kind >= 2:
                low, size = (ROWS // 2 if kind == 3 else 0), ROWS // 2
            target = at_z(cz + step)
        else:
            back = OFFS[kind - 4]
            held = 1 - role if receiving else role
            target = sibling
        where = abuf.at[held * SIDE + mod(cz + back), q, pl.ds(low, size)]
        index = q * 8 + kind
        return pltpu.make_async_remote_copy(
            src_ref=where, dst_ref=where, send_sem=a_send.at[index], recv_sem=a_recv.at[index],
            device_id=target, device_id_type=MESH)

    def p_copy(q):
        return pltpu.make_async_remote_copy(
            src_ref=abuf.at[2 * SIDE, q], dst_ref=abuf.at[SIDE + cz, q],
            send_sem=p_send.at[q], recv_sem=p_recv.at[q],
            device_id=crossed, device_id_type=MESH)

    def c_copy(n):
        return pltpu.make_async_remote_copy(
            src_ref=cout.at[n], dst_ref=cin.at[n], send_sem=c_send.at[n], recv_sem=c_recv.at[n],
            device_id=partner, device_id_type=MESH)

    def state_copy(part, stage, distance, receiving):
        held = (xstate, ystate)[stage]
        position = (cx, cy)[stage]
        index = mod(position - distance) if receiving else position
        target = at_xy(cy, cx + distance) if stage == 0 else at_xy(cy + distance, cx)
        number = part * 6 + stage * 3 + distance - 1
        where = held.at[part, index]
        return pltpu.make_async_remote_copy(
            src_ref=where, dst_ref=where,
            send_sem=s_send.at[number], recv_sem=s_recv.at[number],
            device_id=target, device_id_type=MESH)


    dec[...] = jnp.exp(-rates_ref[...])

    def lanes_of(tile):
        return pl.ds(pl.multiple_of(tile * LANES, LANES), LANES)

    def widen(index):
        in_copy(index).wait()

        def body(tile, carry):
            streams[index, tile, pl.ds(0, PAD), :] = jnp.zeros((PAD, LANES), F32)
            streams[index, tile, pl.ds(PAD, ROWS), :] = inputs[index, :, lanes_of(tile)].astype(F32)
            return carry

        lax.fori_loop(0, TILES, body, 0)

    def widen_halo(index):
        halo_copy(index).wait_recv()
        keep = jnp.where(ctx > 0, 1.0, 0.0).astype(F32)

        def body(tile, carry):
            rim = halo[index, :, lanes_of(tile)].astype(F32)
            streams[index, tile, pl.ds(0, PAD), :] = rim[HALO - PAD:] * keep
            return carry

        lax.fori_loop(0, TILES, body, 0)

    def spread(row):
        return jnp.broadcast_to(row, (SEGS, LANES))

    def strided(index, tile, start):
        return streams[index, tile, pl.ds(start, SEGS, stride=STEPS), :]

    def tap_rows(index, lanes):
        return [spread(taps_ref[index, pl.ds(j, 1), lanes]) for j in range(3)]

    def gate(k_taps, v_taps, k0, k1, k2, v0, v1, v2):
        kf = k_taps[0] * k0 + k_taps[1] * k1 + k_taps[2] * k2
        vf = v_taps[0] * v0 + v_taps[1] * v1 + v_taps[2] * v2
        return kf * vf

    def first_tile(tile, carry):
        lanes = lanes_of(tile)
        decay = [spread(dec[pl.ds(r, 1), lanes]) for r in range(ORDER)]
        k_taps, v_taps = tap_rows(1, lanes), tap_rows(2, lanes)

        def step(i, held):
            k1, k2, v1, v2, states = held
            k0, v0 = strided(1, tile, PAD + i), strided(2, tile, PAD + i)
            gated = gate(k_taps, v_taps, k0, k1, k2, v0, v1, v2)
            gbuf[tile, i] = gated
            states = tuple(decay[r] * states[r] + gated for r in range(ORDER))
            return k0, k1, v0, v1, states

        zero = jnp.zeros((SEGS, LANES), F32)
        start = (strided(1, tile, PAD - 1), strided(1, tile, PAD - 2),
                 strided(2, tile, PAD - 1), strided(2, tile, PAD - 2), (zero,) * ORDER)
        states = lax.fori_loop(0, STEPS, step, start, unroll=4)[4]
        for r in range(ORDER):
            ends[tile, pl.ds(r, SEGS, stride=ORDER), :] = states[r]
        return carry

    def mend_tile(tile, carry):
        lanes = lanes_of(tile)
        k_taps, v_taps = tap_rows(1, lanes), tap_rows(2, lanes)
        k = [strided(1, tile, PAD + d) for d in (-2, -1, 0, 1)]
        v = [strided(2, tile, PAD + d) for d in (-2, -1, 0, 1)]
        changes = []
        for i in (0, 1):
            gated = gate(k_taps, v_taps, k[i + 2], k[i + 1], k[i], v[i + 2], v[i + 1], v[i])
            changes.append(gated - gbuf[tile, i])
            gbuf[tile, i] = gated
        rate = rates_ref[:, lanes]
        far, near = jnp.exp(-float(STEPS - 1) * rate), jnp.exp(-float(STEPS - 2) * rate)
        for r in range(ORDER):
            rows = pl.ds(r, SEGS, stride=ORDER)
            ends[tile, rows, :] = (ends[tile, rows, :] + spread(far[r:r + 1]) * changes[0]
                                   + spread(near[r:r + 1]) * changes[1])
        return carry

    def combine_tile(part):
        def body(tile, carry):
            jump = jnp.exp(-float(STEPS) * rates_ref[:, lanes_of(tile)])
            state = jnp.zeros((ORDER, LANES), F32)
            for seg in range(SEGS):
                inits[tile, pl.ds(seg * ORDER, ORDER), :] = state
                state = jump * state + ends[tile, pl.ds(seg * ORDER, ORDER), :]
            xstate[part, cx, :, lanes_of(tile - part * (TILES // PARTS))] = state
            return carry
        return body

    def row_tile(part):
        def body(tile, carry):
            lanes = lanes_of(tile - part * (TILES // PARTS))
            jump = jnp.exp(-float(ROWS) * rates_ref[:, lanes_of(tile)])
            state = jnp.zeros((ORDER, LANES), F32)
            for position in range(SIDE):
                state = jump * state + xstate[part, position, :, lanes]
            ystate[part, cy, :, lanes] = state
            return carry
        return body

    def seed_tile(part):
        def body(tile, carry):
            lanes = lanes_of(tile - part * (TILES // PARTS))
            rate = rates_ref[:, lanes_of(tile)]
            jump_x = jnp.exp(-float(ROWS) * rate)
            jump_y = jnp.exp(-float(ROWS * SIDE) * rate)
            before_x = jnp.zeros((ORDER, LANES), F32)
            before_y = jnp.zeros((ORDER, LANES), F32)
            for position in range(SIDE - 1):
                before_x = jnp.where(
                    position < cx, jump_x * before_x + xstate[part, position, :, lanes], before_x)
                before_y = jnp.where(
                    position < cy, jump_y * before_y + ystate[part, position, :, lanes], before_y)
            shift = (cx * ROWS).astype(F32)
            state = before_x + jnp.exp(-shift * rate) * before_y
            jump = jnp.exp(-float(STEPS) * rate)
            for seg in range(SEGS):
                rows = pl.ds(seg * ORDER, ORDER)
                inits[tile, rows, :] = inits[tile, rows, :] + state
                state = jump * state
            return carry
        return body

    target_block = jnp.where(role == 0, cz, 2 * SIDE)

    def second_tile(tile, carry):
        lanes = lanes_of(tile)
        decay = [spread(dec[pl.ds(r, 1), lanes]) for r in range(ORDER)]
        weight = [spread(res_ref[pl.ds(r, 1), lanes]) for r in range(ORDER)]
        q_taps = tap_rows(0, lanes)

        def step(i, held):
            q1, q2, states = held
            q0 = strided(0, tile, PAD + i)
            qf = q_taps[0] * q0 + q_taps[1] * q1 + q_taps[2] * q2
            gated = gbuf[tile, i]
            states = tuple(decay[r] * states[r] + gated for r in range(ORDER))
            terms = [weight[r] * states[r] for r in range(ORDER)]
            while len(terms) > 1:
                terms = [terms[j] + terms[j + 1] for j in range(0, len(terms), 2)]
            ybuf[pl.ds(i, SEGS, stride=STEPS), :] = qf * terms[0]
            return q0, q1, states

        start = (strided(0, tile, PAD - 1), strided(0, tile, PAD - 2),
                 tuple(inits[tile, pl.ds(r, SEGS, stride=ORDER), :] for r in range(ORDER)))
        lax.fori_loop(0, STEPS, step, start, unroll=4)
        abuf[target_block, tile // 2, :, lanes_of(tile % 2)] = ybuf[...].astype(BF16)
        return carry

    def tiles(part, body):
        each = TILES // PARTS
        lax.fori_loop(part * each, (part + 1) * each, body, 0)

    def outputs(q):
        lax.fori_loop(2 * q, 2 * q + 2, second_tile, 0)

    def states_out(part, stage):
        for distance in (1, 3, 2):
            state_copy(part, stage, distance, False).start()

    def states_in(part, stage):
        for distance in (1, 3, 2):
            state_copy(part, stage, distance, True).wait_recv()

    def when(wanted, call, *args):
        @pl.when(role == wanted)
        def _():
            call(*args)

    def a_start(q, *kinds):
        for kind in kinds:
            a_copy(q, kind, False).start()

    def p_begin(q):
        p_copy(q).start()

    def a_cross(q):
        p_copy(q).wait_recv()
        a_start(q, 0, 1, 4)

    def a_middle(q):
        for kind in (0, 1):
            a_copy(q, kind, True).wait_recv()
            a_copy(q, kind + 2, False).start()
            a_copy(q, kind + 5, False).start()

    def a_end(q):
        for kind in (2, 3):
            a_copy(q, kind, True).wait_recv()
        a_copy(q, 7, False).start()

    def a_sibling(q, *kinds):
        for kind in kinds:
            a_copy(q, kind, True).wait_recv()

    def a_pair(q):
        a_sibling(q, 4, 5, 6, 7)

    def product(group, n):
        left = jnp.concatenate(
            [abuf[group * SIDE + block, q] for block in range(SIDE) for q in range(PIECES)], 1)
        right = jnp.concatenate([wbuf[j, n] for j in range(2 * SIDE)], 0)
        return jnp.dot(left, right, preferred_element_type=F32)

    def nearby(centre, n, offsets):
        blocks = [mod(centre + offset) for offset in offsets]
        left = jnp.concatenate(
            [abuf[SIDE + block, q] for block in blocks for q in range(PIECES)], 1)
        right = jnp.concatenate([wbuf[block * 2 + j, n] for block in blocks for j in range(2)], 0)
        return jnp.dot(left, right, preferred_element_type=F32)

    def partial(n):
        cout[n] = product(1, n).astype(BF16)

    def prepare(centre, n):
        early[n] = nearby(centre, n, OFFS[:3])

    def finish(centre, n):
        cout[n] = (early[n] + nearby(centre, n, OFFS[3:])).astype(BF16)

    def own(first, count):
        def body(n, carry):
            acc[n] = product(0, n)
            return carry

        lax.fori_loop(first, first + count, body, 0)

    def c_begin(n):
        c_copy(n).start()

    def c_end(n):
        c_copy(n).wait_recv()
        out_ref[:, pl.ds(n * CHUNK, CHUNK)] = (acc[n] + cin[n].astype(F32)).astype(BF16)

    widen(1)
    widen(2)
    widen(0)
    enter()
    w_start(0, 0, 1)
    tiles(0, first_tile)
    widen_halo(1)
    widen_halo(2)
    tiles(0, mend_tile)
    tiles(0, combine_tile(0))
    states_out(0, 0)
    tiles(1, first_tile)
    tiles(1, mend_tile)
    tiles(1, combine_tile(1))
    states_out(1, 0)
    w_start(0, 8, 4)
    widen_halo(0)
    states_in(0, 0)
    tiles(0, row_tile(0))
    states_out(0, 1)
    states_in(1, 0)
    tiles(1, row_tile(1))
    states_out(1, 1)
    w_start(0, 9, 10)
    w_own(1)
    states_in(0, 1)
    tiles(0, seed_tile(0))
    outputs(0)
    when(1, p_begin, 0)
    when(0, a_start, 0, 0, 1, 4)
    outputs(1)
    when(1, p_begin, 1)
    when(0, a_start, 1, 4)
    states_in(1, 1)
    tiles(1, seed_tile(1))
    outputs(2)
    when(1, p_begin, 2)
    when(0, a_start, 2, 4)
    when(1, a_cross, 0)
    outputs(3)
    when(1, p_begin, 3)
    when(0, a_start, 3, 4)
    when(1, a_cross, 1)
    w_first(0)
    when(1, a_middle, 0)
    when(1, a_cross, 2)
    when(1, a_middle, 1)
    when(1, a_cross, 3)
    when(1, a_end, 0)
    when(1, a_middle, 2)
    w_second(0)
    when(1, a_end, 1)
    when(1, a_middle, 3)
    when(0, a_sibling, 3, 4)
    when(0, a_middle, 0)
    when(0, a_start, 1, 0, 1)
    when(0, a_sibling, 0, 4, 5, 6, 7)
    when(0, a_sibling, 1, 4, 5, 6)
    when(0, a_start, 2, 0, 1)
    w_first(1)
    w_own(2)
    when(1, a_end, 2)
    when(1, a_end, 3)
    when(0, a_sibling, 1, 7)
    when(0, a_start, 3, 0, 1)
    w_third(0)
    when(0, a_pair, 2)
    when(0, a_sibling, 3, 5, 6, 7)
    partial(0)
    c_begin(0)
    partial(1)
    c_begin(1)
    when(0, a_middle, 1)
    when(0, a_end, 0)
    w_second(1)
    when(0, a_middle, 2)
    when(0, a_end, 1)
    w_first(2)
    when(0, a_middle, 3)
    w_wait(1, 4, 5, 6)
    prepare(cy, 2)
    w_wait(1, 7, 11, 12, 15, 16)
    finish(cy, 2)
    c_begin(2)
    when(0, a_end, 2)
    when(0, a_end, 3)
    w_second(2)
    w_wait(2, 4, 5, 6)
    prepare(cy, 3)
    w_wait(2, 7, 11, 12, 15, 16)
    finish(cy, 3)
    c_begin(3)
    when(1, a_pair, 0)
    when(1, a_pair, 1)
    when(1, a_pair, 2)
    when(1, a_pair, 3)
    own(0, 4)
    for n in range(CHUNKS):
        c_end(n)

    for n in range(len(GROUPS)):
        for number in range(PER_GROUP):
            w_copy(n, number, False).wait_send()
    for n in range(CHUNKS):
        c_copy(n).wait_send()
    for q in range(PIECES):
        for kind in range(8):
            a_copy(q, kind, False).wait_send()
    for q in range(PARTS):
        for stage in range(2):
            for distance in (1, 2, 3):
                state_copy(q, stage, distance, False).wait_send()

    @pl.when(role == 1)
    def _():
        for q in range(PIECES):
            p_copy(q).wait_send()

    for index in range(3):
        halo_copy(index).wait_send()


def per_device(query, keys_in, values_in, short_taps, mode_rates, mode_residues, out_weight):
    vmem = pl.BlockSpec(memory_space=pltpu.VMEM)
    hbm = pl.BlockSpec(memory_space=pl.ANY)
    dma = pltpu.SemaphoreType.DMA
    return pl.pallas_call(
        kernel,
        out_shape=jax.ShapeDtypeStruct((ROWS, WIDTH), BF16),
        in_specs=[hbm] * 3 + [vmem] * 3 + [hbm],
        out_specs=vmem,
        scratch_shapes=[
            pltpu.VMEM((2 * SIDE, CHUNKS, ROWS, CHUNK), BF16),
            pltpu.VMEM((2 * SIDE + 1, PIECES, ROWS, PIECE), BF16),
            pltpu.VMEM((CHUNKS, ROWS, CHUNK), F32),
            pltpu.VMEM((CHUNKS, ROWS, CHUNK), F32),
            pltpu.VMEM((CHUNKS, ROWS, CHUNK), BF16),
            pltpu.VMEM((CHUNKS, ROWS, CHUNK), BF16),
            pltpu.VMEM((3, ROWS, WIDTH), BF16),
            pltpu.VMEM((3, TILES, PAD + ROWS, LANES), F32),
            pltpu.VMEM((TILES, STEPS, SEGS, LANES), F32),
            pltpu.VMEM((ROWS, LANES), F32),
            pltpu.VMEM((3, HALO, WIDTH), BF16),
            pltpu.VMEM((ORDER, WIDTH), F32),
            pltpu.VMEM((TILES, SEGS * ORDER, LANES), F32),
            pltpu.VMEM((TILES, SEGS * ORDER, LANES), F32),
            pltpu.VMEM((PARTS, SIDE, ORDER, PART), F32),
            pltpu.VMEM((PARTS, SIDE, ORDER, PART), F32),
            dma((len(GROUPS) * PER_GROUP,)), dma((len(GROUPS) * PER_GROUP,)),
            dma((PIECES * 8,)), dma((PIECES * 8,)), dma((PIECES,)), dma((PIECES,)),
            dma((CHUNKS,)), dma((CHUNKS,)), dma((3,)), dma((3,)),
            dma((PARTS * 6,)), dma((PARTS * 6,)), dma((CHUNKS,)), dma((3,)),
        ],
        compiler_params=pltpu.CompilerParams(
            collective_id=0, has_side_effects=True, vmem_limit_bytes=56 * 1024 * 1024),
        cost_estimate=pl.CostEstimate(
            flops=2 * ROWS * 8192 * WIDTH, bytes_accessed=6 * 1024 * 1024, transcendentals=0),
    )(query, keys_in, values_in, short_taps, mode_rates, mode_residues, out_weight)


def solution(mesh):
    in_specs = (
        P("ctx", "ch"),
        P("ctx", "ch"),
        P("ctx", "ch"),
        P(None, None, "ch"),
        P(None, "ch"),
        P(None, "ch"),
        P("ctx", "ch"),
    )
    return jax.shard_map(
        per_device, mesh=mesh, in_specs=in_specs, out_specs=P("ctx", "ch"), check_vma=False
    )
```

```python
import jax
import jax.numpy as jnp
from jax import lax
from jax.experimental import pallas as pl
from jax.experimental.pallas import tpu as pltpu
from jax.sharding import PartitionSpec as P

MESH = pl.DeviceIdType.MESH
SIDE = 4
ORDER = 16
ROWS = 512
WIDTH = 1024
LANES = 128
TILES = WIDTH // LANES
SEGS = 8
STEPS = ROWS // SEGS
PAD = 8
HALO = 16
PARTS = 2
PART = WIDTH // PARTS
PIECES = 4
PIECE = WIDTH // PIECES
CHUNKS = 4
CHUNK = WIDTH // CHUNKS
CUT = 224
OFFS = (0, -1, 1, 2)
PER_GROUP = 17
GROUPS = ((0, 2), (2, 1), (3, 1))
F32 = jnp.float32
BF16 = jnp.bfloat16


def kernel(
    q_hbm, k_hbm, v_hbm, taps_ref, rates_ref, res_ref, w_ref, out_ref,
    wbuf, abuf, acc, early, cout, cin, inputs, streams, gbuf, ybuf, halo, dec, ends, inits, xstate, ystate,
    w_send, w_recv, a_send, a_recv, p_send, p_recv, c_send, c_recv, h_send, h_recv, s_send, s_recv,
    own_sem, in_sem,
):
    ctx = lax.axis_index("ctx")
    ch = lax.axis_index("ch")
    cy, cx = ctx // SIDE, ctx % SIDE
    cz, core = ch // 2, ch % 2
    column, side = cx % 2, cx // 2
    role = jnp.where(core == side, 0, 1)

    def mod(value):
        return lax.rem(value + 2 * SIDE, SIDE)

    def at_xy(y, x):
        return (mod(y) * SIDE + mod(x), ch)

    following = (lax.rem(ctx + 1, SIDE * SIDE), ch)
    previous = (lax.rem(ctx + SIDE * SIDE - 1, SIDE * SIDE), ch)
    sibling = (ctx, cz * 2 + 1 - core)
    beside = at_xy(cy, cx + 1 - 2 * column)
    partner = at_xy(cy, 3 - cx)
    crossed = (cy * SIDE + 3 - cx, cz * 2 + 1 - core)

    def at_z(z):
        return (ctx, mod(z) * 2 + core)

    barrier = pltpu.get_barrier_semaphore()
    others = [at_xy(cy, cx + d) for d in (1, 2, 3)] + [at_xy(cy + d, cx) for d in (1, 2, 3)]
    others += [at_z(cz + 1), at_z(cz - 1), sibling, following, previous, crossed]
    for other in others:
        pl.semaphore_signal(barrier, inc=1, device_id=other, device_id_type=MESH)

    sources = (q_hbm, k_hbm, v_hbm)

    def own_copy(n):
        return pltpu.make_async_copy(
            w_ref.at[:, pl.ds(n * CHUNK, CHUNK)], wbuf.at[cy * 2 + column, n], own_sem.at[n])

    def in_copy(index):
        return pltpu.make_async_copy(sources[index], inputs.at[index], in_sem.at[index])

    for n in range(CHUNKS):
        own_copy(n).start()
    for index in (1, 2, 0):
        in_copy(index).start()
    def halo_copy(index):
        return pltpu.make_async_remote_copy(
            src_ref=sources[index].at[pl.ds(ROWS - HALO, HALO)], dst_ref=halo.at[index],
            send_sem=h_send.at[index], recv_sem=h_recv.at[index],
            device_id=following, device_id_type=MESH)

    def enter():
        pl.semaphore_wait(barrier, len(others))
        for index in (1, 2, 0):
            halo_copy(index).start()
        for n in range(CHUNKS):
            own_copy(n).wait()

    def ring(kind, receiving):
        step = 1 if kind % 2 == 0 else -1
        if receiving:
            return step, (-step if kind < 2 else -2 * step)
        return step, (0 if kind < 2 else -step)

    def w_copy(n, number, receiving):
        if number < 4 or number >= 9:
            kind = number if number < 4 else (number - 9) % 4
            step, back = ring(kind, receiving)
            row = cy + back
            flip = number >= 13
            target = at_xy(cy + step, cx)
            low, high = (0, CUT) if number < 4 else (CUT, ROWS)
            middle = (low + high) // 2
            if kind == 2:
                high = middle
            if kind == 3:
                low = middle
        else:
            row = cy + (OFFS[number - 4] if number < 8 else 0)
            flip = receiving
            target = beside
            low, high = (0, CUT) if number < 8 else (CUT, ROWS)
        across = 1 - column if flip else column
        where = wbuf.at[mod(row) * 2 + across, pl.ds(*GROUPS[n]), pl.ds(low, high - low)]
        index = n * PER_GROUP + number
        return pltpu.make_async_remote_copy(
            src_ref=where, dst_ref=where, send_sem=w_send.at[index], recv_sem=w_recv.at[index],
            device_id=target, device_id_type=MESH)

    def w_start(n, *numbers):
        for number in numbers:
            w_copy(n, number, False).start()

    def w_wait(n, *numbers):
        for number in numbers:
            w_copy(n, number, True).wait_recv()

    def w_own(n):
        w_start(n, 8, 0, 1, 9, 10, 4)

    def w_first(n):
        w_wait(n, 8)
        w_start(n, 13, 14)
        for kind in (0, 1):
            w_wait(n, kind)
            w_start(n, kind + 2, 5 + kind)
        for kind in (0, 1):
            w_wait(n, 9 + kind)
            w_start(n, 11 + kind)

    def w_second(n):
        w_wait(n, 2, 3)
        w_start(n, 7)
        for kind in (0, 1):
            w_wait(n, 13 + kind)
            w_start(n, 15 + kind)

    def w_third(n):
        w_wait(n, 4, 5, 6, 7, 11, 12, 15, 16)

    def a_copy(q, kind, receiving):
        low, size = 0, ROWS
        held = role
        if kind < 4:
            step, back = ring(kind, receiving)
            if kind >= 2:
                low, size = (ROWS // 2 if kind == 3 else 0), ROWS // 2
            target = at_z(cz + step)
        else:
            back = OFFS[kind - 4]
            held = 1 - role if receiving else role
            target = sibling
        where = abuf.at[held * SIDE + mod(cz + back), q, pl.ds(low, size)]
        index = q * 8 + kind
        return pltpu.make_async_remote_copy(
            src_ref=where, dst_ref=where, send_sem=a_send.at[index], recv_sem=a_recv.at[index],
            device_id=target, device_id_type=MESH)

    def p_copy(q):
        return pltpu.make_async_remote_copy(
            src_ref=abuf.at[2 * SIDE, q], dst_ref=abuf.at[SIDE + cz, q],
            send_sem=p_send.at[q], recv_sem=p_recv.at[q],
            device_id=crossed, device_id_type=MESH)

    def c_copy(n):
        return pltpu.make_async_remote_copy(
            src_ref=cout.at[n], dst_ref=cin.at[n], send_sem=c_send.at[n], recv_sem=c_recv.at[n],
            device_id=partner, device_id_type=MESH)

    def state_copy(part, stage, distance, receiving):
        held = (xstate, ystate)[stage]
        position = (cx, cy)[stage]
        index = mod(position - distance) if receiving else position
        target = at_xy(cy, cx + distance) if stage == 0 else at_xy(cy + distance, cx)
        number = part * 6 + stage * 3 + distance - 1
        where = held.at[part, index]
        return pltpu.make_async_remote_copy(
            src_ref=where, dst_ref=where,
            send_sem=s_send.at[number], recv_sem=s_recv.at[number],
            device_id=target, device_id_type=MESH)


    dec[...] = jnp.exp(-rates_ref[...])

    def lanes_of(tile):
        return pl.ds(pl.multiple_of(tile * LANES, LANES), LANES)

    def widen(index):
        in_copy(index).wait()

        def body(tile, carry):
            streams[index, tile, pl.ds(0, PAD), :] = jnp.zeros((PAD, LANES), F32)
            streams[index, tile, pl.ds(PAD, ROWS), :] = inputs[index, :, lanes_of(tile)].astype(F32)
            return carry

        lax.fori_loop(0, TILES, body, 0)

    def widen_halo(index):
        halo_copy(index).wait_recv()
        keep = jnp.where(ctx > 0, 1.0, 0.0).astype(F32)

        def body(tile, carry):
            rim = halo[index, :, lanes_of(tile)].astype(F32)
            streams[index, tile, pl.ds(0, PAD), :] = rim[HALO - PAD:] * keep
            return carry

        lax.fori_loop(0, TILES, body, 0)

    def spread(row):
        return jnp.broadcast_to(row, (SEGS, LANES))

    def strided(index, tile, start):
        return streams[index, tile, pl.ds(start, SEGS, stride=STEPS), :]

    def tap_rows(index, lanes):
        return [spread(taps_ref[index, pl.ds(j, 1), lanes]) for j in range(3)]

    def gate(k_taps, v_taps, k0, k1, k2, v0, v1, v2):
        kf = k_taps[0] * k0 + k_taps[1] * k1 + k_taps[2] * k2
        vf = v_taps[0] * v0 + v_taps[1] * v1 + v_taps[2] * v2
        return kf * vf

    def first_tile(tile, carry):
        lanes = lanes_of(tile)
        decay = [spread(dec[pl.ds(r, 1), lanes]) for r in range(ORDER)]
        k_taps, v_taps = tap_rows(1, lanes), tap_rows(2, lanes)

        def step(i, held):
            k1, k2, v1, v2, states = held
            k0, v0 = strided(1, tile, PAD + i), strided(2, tile, PAD + i)
            gated = gate(k_taps, v_taps, k0, k1, k2, v0, v1, v2)
            gbuf[tile, i] = gated
            states = tuple(decay[r] * states[r] + gated for r in range(ORDER))
            return k0, k1, v0, v1, states

        zero = jnp.zeros((SEGS, LANES), F32)
        start = (strided(1, tile, PAD - 1), strided(1, tile, PAD - 2),
                 strided(2, tile, PAD - 1), strided(2, tile, PAD - 2), (zero,) * ORDER)
        states = lax.fori_loop(0, STEPS, step, start, unroll=4)[4]
        for r in range(ORDER):
            ends[tile, pl.ds(r, SEGS, stride=ORDER), :] = states[r]
        return carry

    def mend_tile(tile, carry):
        lanes = lanes_of(tile)
        k_taps, v_taps = tap_rows(1, lanes), tap_rows(2, lanes)
        k = [strided(1, tile, PAD + d) for d in (-2, -1, 0, 1)]
        v = [strided(2, tile, PAD + d) for d in (-2, -1, 0, 1)]
        changes = []
        for i in (0, 1):
            gated = gate(k_taps, v_taps, k[i + 2], k[i + 1], k[i], v[i + 2], v[i + 1], v[i])
            changes.append(gated - gbuf[tile, i])
            gbuf[tile, i] = gated
        rate = rates_ref[:, lanes]
        far, near = jnp.exp(-float(STEPS - 1) * rate), jnp.exp(-float(STEPS - 2) * rate)
        for r in range(ORDER):
            rows = pl.ds(r, SEGS, stride=ORDER)
            ends[tile, rows, :] = (ends[tile, rows, :] + spread(far[r:r + 1]) * changes[0]
                                   + spread(near[r:r + 1]) * changes[1])
        return carry

    def combine_tile(part):
        def body(tile, carry):
            jump = jnp.exp(-float(STEPS) * rates_ref[:, lanes_of(tile)])
            state = jnp.zeros((ORDER, LANES), F32)
            for seg in range(SEGS):
                inits[tile, pl.ds(seg * ORDER, ORDER), :] = state
                state = jump * state + ends[tile, pl.ds(seg * ORDER, ORDER), :]
            xstate[part, cx, :, lanes_of(tile - part * (TILES // PARTS))] = state
            return carry
        return body

    def row_tile(part):
        def body(tile, carry):
            lanes = lanes_of(tile - part * (TILES // PARTS))
            jump = jnp.exp(-float(ROWS) * rates_ref[:, lanes_of(tile)])
            state = jnp.zeros((ORDER, LANES), F32)
            for position in range(SIDE):
                state = jump * state + xstate[part, position, :, lanes]
            ystate[part, cy, :, lanes] = state
            return carry
        return body

    def seed_tile(part):
        def body(tile, carry):
            lanes = lanes_of(tile - part * (TILES // PARTS))
            rate = rates_ref[:, lanes_of(tile)]
            jump_x = jnp.exp(-float(ROWS) * rate)
            jump_y = jnp.exp(-float(ROWS * SIDE) * rate)
            before_x = jnp.zeros((ORDER, LANES), F32)
            before_y = jnp.zeros((ORDER, LANES), F32)
            for position in range(SIDE - 1):
                before_x = jnp.where(
                    position < cx, jump_x * before_x + xstate[part, position, :, lanes], before_x)
                before_y = jnp.where(
                    position < cy, jump_y * before_y + ystate[part, position, :, lanes], before_y)
            shift = (cx * ROWS).astype(F32)
            state = before_x + jnp.exp(-shift * rate) * before_y
            jump = jnp.exp(-float(STEPS) * rate)
            for seg in range(SEGS):
                rows = pl.ds(seg * ORDER, ORDER)
                inits[tile, rows, :] = inits[tile, rows, :] + state
                state = jump * state
            return carry
        return body

    target_block = jnp.where(role == 0, cz, 2 * SIDE)

    def second_tile(tile, carry):
        lanes = lanes_of(tile)
        decay = [spread(dec[pl.ds(r, 1), lanes]) for r in range(ORDER)]
        weight = [spread(res_ref[pl.ds(r, 1), lanes]) for r in range(ORDER)]
        q_taps = tap_rows(0, lanes)

        def step(i, held):
            q1, q2, states = held
            q0 = strided(0, tile, PAD + i)
            qf = q_taps[0] * q0 + q_taps[1] * q1 + q_taps[2] * q2
            gated = gbuf[tile, i]
            states = tuple(decay[r] * states[r] + gated for r in range(ORDER))
            terms = [weight[r] * states[r] for r in range(ORDER)]
            while len(terms) > 1:
                terms = [terms[j] + terms[j + 1] for j in range(0, len(terms), 2)]
            ybuf[pl.ds(i, SEGS, stride=STEPS), :] = qf * terms[0]
            return q0, q1, states

        start = (strided(0, tile, PAD - 1), strided(0, tile, PAD - 2),
                 tuple(inits[tile, pl.ds(r, SEGS, stride=ORDER), :] for r in range(ORDER)))
        lax.fori_loop(0, STEPS, step, start, unroll=4)
        abuf[target_block, tile // 2, :, lanes_of(tile % 2)] = ybuf[...].astype(BF16)
        return carry

    def tiles(part, body):
        each = TILES // PARTS
        lax.fori_loop(part * each, (part + 1) * each, body, 0)

    def outputs(q):
        lax.fori_loop(2 * q, 2 * q + 2, second_tile, 0)

    def states_out(part, stage):
        for distance in (1, 3, 2):
            state_copy(part, stage, distance, False).start()

    def states_in(part, stage):
        for distance in (1, 3, 2):
            state_copy(part, stage, distance, True).wait_recv()

    def when(wanted, call, *args):
        @pl.when(role == wanted)
        def _():
            call(*args)

    def a_start(q, *kinds):
        for kind in kinds:
            a_copy(q, kind, False).start()

    def p_begin(q):
        p_copy(q).start()

    def a_cross(q):
        p_copy(q).wait_recv()
        a_start(q, 0, 1, 4)

    def a_middle(q):
        for kind in (0, 1):
            a_copy(q, kind, True).wait_recv()
            a_copy(q, kind + 2, False).start()
            a_copy(q, kind + 5, False).start()

    def a_end(q):
        for kind in (2, 3):
            a_copy(q, kind, True).wait_recv()
        a_copy(q, 7, False).start()

    def a_sibling(q, *kinds):
        for kind in kinds:
            a_copy(q, kind, True).wait_recv()

    def a_pair(q):
        a_sibling(q, 4, 5, 6, 7)

    def product(group, n):
        left = jnp.concatenate(
            [abuf[group * SIDE + block, q] for block in range(SIDE) for q in range(PIECES)], 1)
        right = jnp.concatenate([wbuf[j, n] for j in range(2 * SIDE)], 0)
        return jnp.dot(left, right, preferred_element_type=F32)

    def nearby(centre, n, offsets):
        blocks = [mod(centre + offset) for offset in offsets]
        left = jnp.concatenate(
            [abuf[SIDE + block, q] for block in blocks for q in range(PIECES)], 1)
        right = jnp.concatenate([wbuf[block * 2 + j, n] for block in blocks for j in range(2)], 0)
        return jnp.dot(left, right, preferred_element_type=F32)

    def partial(n):
        cout[n] = product(1, n).astype(BF16)

    def prepare(centre, n):
        early[n] = nearby(centre, n, OFFS[:3])

    def finish(centre, n):
        cout[n] = (early[n] + nearby(centre, n, OFFS[3:])).astype(BF16)

    def own(first, count):
        def body(n, carry):
            acc[n] = product(0, n)
            return carry

        lax.fori_loop(first, first + count, body, 0)

    def c_begin(n):
        c_copy(n).start()

    def c_end(n):
        c_copy(n).wait_recv()
        out_ref[:, pl.ds(n * CHUNK, CHUNK)] = (acc[n] + cin[n].astype(F32)).astype(BF16)

    widen(1)
    widen(2)
    enter()
    w_start(0, 0, 1)
    tiles(0, first_tile)
    widen_halo(1)
    widen_halo(2)
    tiles(0, mend_tile)
    tiles(0, combine_tile(0))
    states_out(0, 0)
    tiles(1, first_tile)
    tiles(1, mend_tile)
    tiles(1, combine_tile(1))
    states_out(1, 0)
    w_start(0, 8, 4)
    widen(0)
    widen_halo(0)
    states_in(0, 0)
    tiles(0, row_tile(0))
    states_out(0, 1)
    states_in(1, 0)
    tiles(1, row_tile(1))
    states_out(1, 1)
    w_start(0, 9, 10)
    w_own(1)
    states_in(0, 1)
    tiles(0, seed_tile(0))
    outputs(0)
    when(1, p_begin, 0)
    when(0, a_start, 0, 0, 1, 4)
    outputs(1)
    when(1, p_begin, 1)
    when(0, a_start, 1, 0, 1, 4)
    states_in(1, 1)
    tiles(1, seed_tile(1))
    outputs(2)
    when(1, p_begin, 2)
    when(0, a_start, 2, 4)
    when(1, a_cross, 0)
    outputs(3)
    when(1, p_begin, 3)
    when(0, a_start, 3, 4)
    when(1, a_cross, 1)
    w_first(0)
    when(1, a_middle, 0)
    when(1, a_cross, 2)
    when(1, a_middle, 1)
    when(1, a_cross, 3)
    when(1, a_end, 0)
    when(1, a_middle, 2)
    w_second(0)
    when(1, a_end, 1)
    when(1, a_middle, 3)
    when(0, a_middle, 0)
    when(0, a_sibling, 3, 4)
    when(0, a_sibling, 0, 4, 5, 6, 7)
    when(0, a_sibling, 1, 4, 5, 6)
    when(0, a_start, 2, 0, 1)
    w_first(1)
    w_own(2)
    when(1, a_end, 2)
    when(1, a_end, 3)
    when(0, a_sibling, 1, 7)
    when(0, a_start, 3, 0, 1)
    w_third(0)
    when(0, a_pair, 2)
    when(0, a_sibling, 3, 5, 6, 7)
    partial(0)
    c_begin(0)
    partial(1)
    c_begin(1)
    when(0, a_middle, 1)
    when(0, a_end, 0)
    w_second(1)
    when(0, a_middle, 2)
    when(0, a_end, 1)
    w_first(2)
    when(0, a_middle, 3)
    w_wait(1, 4, 5, 6)
    prepare(cy, 2)
    w_wait(1, 7, 11, 12, 15, 16)
    finish(cy, 2)
    c_begin(2)
    when(0, a_end, 2)
    when(0, a_end, 3)
    w_second(2)
    w_wait(2, 4, 5, 6)
    prepare(cy, 3)
    w_wait(2, 7, 11, 12, 15, 16)
    finish(cy, 3)
    c_begin(3)
    when(1, a_pair, 0)
    when(1, a_pair, 1)
    when(1, a_pair, 2)
    when(1, a_pair, 3)
    own(0, 4)
    for n in range(CHUNKS):
        c_end(n)

    for n in range(len(GROUPS)):
        for number in range(PER_GROUP):
            w_copy(n, number, False).wait_send()
    for n in range(CHUNKS):
        c_copy(n).wait_send()
    for q in range(PIECES):
        for kind in range(8):
            a_copy(q, kind, False).wait_send()
    for q in range(PARTS):
        for stage in range(2):
            for distance in (1, 2, 3):
                state_copy(q, stage, distance, False).wait_send()

    @pl.when(role == 1)
    def _():
        for q in range(PIECES):
            p_copy(q).wait_send()

    for index in range(3):
        halo_copy(index).wait_send()


def per_device(query, keys_in, values_in, short_taps, mode_rates, mode_residues, out_weight):
    vmem = pl.BlockSpec(memory_space=pltpu.VMEM)
    hbm = pl.BlockSpec(memory_space=pl.ANY)
    dma = pltpu.SemaphoreType.DMA
    return pl.pallas_call(
        kernel,
        out_shape=jax.ShapeDtypeStruct((ROWS, WIDTH), BF16),
        in_specs=[hbm] * 3 + [vmem] * 3 + [hbm],
        out_specs=vmem,
        scratch_shapes=[
            pltpu.VMEM((2 * SIDE, CHUNKS, ROWS, CHUNK), BF16),
            pltpu.VMEM((2 * SIDE + 1, PIECES, ROWS, PIECE), BF16),
            pltpu.VMEM((CHUNKS, ROWS, CHUNK), F32),
            pltpu.VMEM((CHUNKS, ROWS, CHUNK), F32),
            pltpu.VMEM((CHUNKS, ROWS, CHUNK), BF16),
            pltpu.VMEM((CHUNKS, ROWS, CHUNK), BF16),
            pltpu.VMEM((3, ROWS, WIDTH), BF16),
            pltpu.VMEM((3, TILES, PAD + ROWS, LANES), F32),
            pltpu.VMEM((TILES, STEPS, SEGS, LANES), F32),
            pltpu.VMEM((ROWS, LANES), F32),
            pltpu.VMEM((3, HALO, WIDTH), BF16),
            pltpu.VMEM((ORDER, WIDTH), F32),
            pltpu.VMEM((TILES, SEGS * ORDER, LANES), F32),
            pltpu.VMEM((TILES, SEGS * ORDER, LANES), F32),
            pltpu.VMEM((PARTS, SIDE, ORDER, PART), F32),
            pltpu.VMEM((PARTS, SIDE, ORDER, PART), F32),
            dma((len(GROUPS) * PER_GROUP,)), dma((len(GROUPS) * PER_GROUP,)),
            dma((PIECES * 8,)), dma((PIECES * 8,)), dma((PIECES,)), dma((PIECES,)),
            dma((CHUNKS,)), dma((CHUNKS,)), dma((3,)), dma((3,)),
            dma((PARTS * 6,)), dma((PARTS * 6,)), dma((CHUNKS,)), dma((3,)),
        ],
        compiler_params=pltpu.CompilerParams(
            collective_id=0, has_side_effects=True, vmem_limit_bytes=56 * 1024 * 1024),
        cost_estimate=pl.CostEstimate(
            flops=2 * ROWS * 8192 * WIDTH, bytes_accessed=6 * 1024 * 1024, transcendentals=0),
    )(query, keys_in, values_in, short_taps, mode_rates, mode_residues, out_weight)


def solution(mesh):
    in_specs = (
        P("ctx", "ch"),
        P("ctx", "ch"),
        P("ctx", "ch"),
        P(None, None, "ch"),
        P(None, "ch"),
        P(None, "ch"),
        P("ctx", "ch"),
    )
    return jax.shard_map(
        per_device, mesh=mesh, in_specs=in_specs, out_specs=P("ctx", "ch"), check_vma=False
    )
```

```python
import jax
import jax.numpy as jnp
from jax import lax
from jax.experimental import pallas as pl
from jax.experimental.pallas import tpu as pltpu
from jax.sharding import PartitionSpec as P

MESH = pl.DeviceIdType.MESH
SIDE = 4
ORDER = 16
ROWS = 512
WIDTH = 1024
LANES = 128
TILES = WIDTH // LANES
SEGS = 8
STEPS = ROWS // SEGS
PAD = 8
HALO = 16
PARTS = 2
PART = WIDTH // PARTS
PIECES = 4
PIECE = WIDTH // PIECES
CHUNKS = 4
CHUNK = WIDTH // CHUNKS
CUT = 224
OFFS = (0, -1, 1, 2)
PER_GROUP = 17
GROUPS = ((0, 2), (2, 1), (3, 1))
F32 = jnp.float32
BF16 = jnp.bfloat16


def kernel(
    q_hbm, k_hbm, v_hbm, taps_ref, rates_ref, res_ref, w_ref, out_ref,
    wbuf, abuf, acc, early, cout, cin, inputs, streams, gbuf, ybuf, halo, dec, ends, inits, xstate, ystate,
    w_send, w_recv, a_send, a_recv, p_send, p_recv, c_send, c_recv, h_send, h_recv, s_send, s_recv,
    own_sem, in_sem,
):
    ctx = lax.axis_index("ctx")
    ch = lax.axis_index("ch")
    cy, cx = ctx // SIDE, ctx % SIDE
    cz, core = ch // 2, ch % 2
    column, side = cx % 2, cx // 2
    role = jnp.where(core == side, 0, 1)

    def mod(value):
        return lax.rem(value + 2 * SIDE, SIDE)

    def at_xy(y, x):
        return (mod(y) * SIDE + mod(x), ch)

    following = (lax.rem(ctx + 1, SIDE * SIDE), ch)
    previous = (lax.rem(ctx + SIDE * SIDE - 1, SIDE * SIDE), ch)
    sibling = (ctx, cz * 2 + 1 - core)
    beside = at_xy(cy, cx + 1 - 2 * column)
    partner = at_xy(cy, 3 - cx)
    crossed = (cy * SIDE + 3 - cx, cz * 2 + 1 - core)

    def at_z(z):
        return (ctx, mod(z) * 2 + core)

    barrier = pltpu.get_barrier_semaphore()
    others = [at_xy(cy, cx + d) for d in (1, 2, 3)] + [at_xy(cy + d, cx) for d in (1, 2, 3)]
    others += [at_z(cz + 1), at_z(cz - 1), sibling, following, previous, crossed]
    for other in others:
        pl.semaphore_signal(barrier, inc=1, device_id=other, device_id_type=MESH)

    sources = (q_hbm, k_hbm, v_hbm)

    def own_copy(n):
        return pltpu.make_async_copy(
            w_ref.at[:, pl.ds(n * CHUNK, CHUNK)], wbuf.at[cy * 2 + column, n], own_sem.at[n])

    def in_copy(index):
        return pltpu.make_async_copy(sources[index], inputs.at[index], in_sem.at[index])

    for n in range(CHUNKS):
        own_copy(n).start()
    for index in (1, 2, 0):
        in_copy(index).start()
    def halo_copy(index):
        return pltpu.make_async_remote_copy(
            src_ref=sources[index].at[pl.ds(ROWS - HALO, HALO)], dst_ref=halo.at[index],
            send_sem=h_send.at[index], recv_sem=h_recv.at[index],
            device_id=following, device_id_type=MESH)

    def enter():
        pl.semaphore_wait(barrier, len(others))
        for index in (1, 2, 0):
            halo_copy(index).start()
        for n in range(CHUNKS):
            own_copy(n).wait()

    def ring(kind, receiving):
        step = 1 if kind % 2 == 0 else -1
        if receiving:
            return step, (-step if kind < 2 else -2 * step)
        return step, (0 if kind < 2 else -step)

    def w_copy(n, number, receiving):
        if number < 4 or number >= 9:
            kind = number if number < 4 else (number - 9) % 4
            step, back = ring(kind, receiving)
            row = cy + back
            flip = number >= 13
            target = at_xy(cy + step, cx)
            low, high = (0, CUT) if number < 4 else (CUT, ROWS)
            middle = (low + high) // 2
            if kind == 2:
                high = middle
            if kind == 3:
                low = middle
        else:
            row = cy + (OFFS[number - 4] if number < 8 else 0)
            flip = receiving
            target = beside
            low, high = (0, CUT) if number < 8 else (CUT, ROWS)
        across = 1 - column if flip else column
        where = wbuf.at[mod(row) * 2 + across, pl.ds(*GROUPS[n]), pl.ds(low, high - low)]
        index = n * PER_GROUP + number
        return pltpu.make_async_remote_copy(
            src_ref=where, dst_ref=where, send_sem=w_send.at[index], recv_sem=w_recv.at[index],
            device_id=target, device_id_type=MESH)

    def w_start(n, *numbers):
        for number in numbers:
            w_copy(n, number, False).start()

    def w_wait(n, *numbers):
        for number in numbers:
            w_copy(n, number, True).wait_recv()

    def w_own(n):
        w_start(n, 8, 0, 1, 9, 10, 4)

    def w_first(n):
        w_wait(n, 8)
        w_start(n, 13, 14)
        for kind in (0, 1):
            w_wait(n, kind)
            w_start(n, kind + 2, 5 + kind)
        for kind in (0, 1):
            w_wait(n, 9 + kind)
            w_start(n, 11 + kind)

    def w_second(n):
        w_wait(n, 2, 3)
        w_start(n, 7)
        for kind in (0, 1):
            w_wait(n, 13 + kind)
            w_start(n, 15 + kind)

    def w_third(n):
        w_wait(n, 4, 5, 6, 7, 11, 12, 15, 16)

    def a_copy(q, kind, receiving):
        low, size = 0, ROWS
        held = role
        if kind < 4:
            step, back = ring(kind, receiving)
            if kind >= 2:
                low, size = (ROWS // 2 if kind == 3 else 0), ROWS // 2
            target = at_z(cz + step)
        else:
            back = OFFS[kind - 4]
            held = 1 - role if receiving else role
            target = sibling
        where = abuf.at[held * SIDE + mod(cz + back), q, pl.ds(low, size)]
        index = q * 8 + kind
        return pltpu.make_async_remote_copy(
            src_ref=where, dst_ref=where, send_sem=a_send.at[index], recv_sem=a_recv.at[index],
            device_id=target, device_id_type=MESH)

    def p_copy(q):
        return pltpu.make_async_remote_copy(
            src_ref=abuf.at[2 * SIDE, q], dst_ref=abuf.at[SIDE + cz, q],
            send_sem=p_send.at[q], recv_sem=p_recv.at[q],
            device_id=crossed, device_id_type=MESH)

    def c_copy(n):
        return pltpu.make_async_remote_copy(
            src_ref=cout.at[n], dst_ref=cin.at[n], send_sem=c_send.at[n], recv_sem=c_recv.at[n],
            device_id=partner, device_id_type=MESH)

    def state_copy(part, stage, distance, receiving):
        held = (xstate, ystate)[stage]
        position = (cx, cy)[stage]
        index = mod(position - distance) if receiving else position
        target = at_xy(cy, cx + distance) if stage == 0 else at_xy(cy + distance, cx)
        number = part * 6 + stage * 3 + distance - 1
        where = held.at[part, index]
        return pltpu.make_async_remote_copy(
            src_ref=where, dst_ref=where,
            send_sem=s_send.at[number], recv_sem=s_recv.at[number],
            device_id=target, device_id_type=MESH)


    dec[...] = jnp.exp(-rates_ref[...])

    def lanes_of(tile):
        return pl.ds(pl.multiple_of(tile * LANES, LANES), LANES)

    def widen(index):
        in_copy(index).wait()

        def body(tile, carry):
            streams[index, tile, pl.ds(0, PAD), :] = jnp.zeros((PAD, LANES), F32)
            streams[index, tile, pl.ds(PAD, ROWS), :] = inputs[index, :, lanes_of(tile)].astype(F32)
            return carry

        lax.fori_loop(0, TILES, body, 0)

    def widen_halo(index):
        halo_copy(index).wait_recv()
        keep = jnp.where(ctx > 0, 1.0, 0.0).astype(F32)

        def body(tile, carry):
            rim = halo[index, :, lanes_of(tile)].astype(F32)
            streams[index, tile, pl.ds(0, PAD), :] = rim[HALO - PAD:] * keep
            return carry

        lax.fori_loop(0, TILES, body, 0)

    def spread(row):
        return jnp.broadcast_to(row, (SEGS, LANES))

    def strided(index, tile, start):
        return streams[index, tile, pl.ds(start, SEGS, stride=STEPS), :]

    def tap_rows(index, lanes):
        return [spread(taps_ref[index, pl.ds(j, 1), lanes]) for j in range(3)]

    def gate(k_taps, v_taps, k0, k1, k2, v0, v1, v2):
        kf = k_taps[0] * k0 + k_taps[1] * k1 + k_taps[2] * k2
        vf = v_taps[0] * v0 + v_taps[1] * v1 + v_taps[2] * v2
        return kf * vf

    def first_tile(tile, carry):
        lanes = lanes_of(tile)
        decay = [spread(dec[pl.ds(r, 1), lanes]) for r in range(ORDER)]
        k_taps, v_taps = tap_rows(1, lanes), tap_rows(2, lanes)

        def step(i, held):
            k1, k2, v1, v2, states = held
            k0, v0 = strided(1, tile, PAD + i), strided(2, tile, PAD + i)
            gated = gate(k_taps, v_taps, k0, k1, k2, v0, v1, v2)
            gbuf[tile, i] = gated
            states = tuple(decay[r] * states[r] + gated for r in range(ORDER))
            return k0, k1, v0, v1, states

        zero = jnp.zeros((SEGS, LANES), F32)
        start = (strided(1, tile, PAD - 1), strided(1, tile, PAD - 2),
                 strided(2, tile, PAD - 1), strided(2, tile, PAD - 2), (zero,) * ORDER)
        states = lax.fori_loop(0, STEPS, step, start, unroll=4)[4]
        for r in range(ORDER):
            ends[tile, pl.ds(r, SEGS, stride=ORDER), :] = states[r]
        return carry

    def mend_tile(tile, carry):
        lanes = lanes_of(tile)
        k_taps, v_taps = tap_rows(1, lanes), tap_rows(2, lanes)
        k = [strided(1, tile, PAD + d) for d in (-2, -1, 0, 1)]
        v = [strided(2, tile, PAD + d) for d in (-2, -1, 0, 1)]
        changes = []
        for i in (0, 1):
            gated = gate(k_taps, v_taps, k[i + 2], k[i + 1], k[i], v[i + 2], v[i + 1], v[i])
            changes.append(gated - gbuf[tile, i])
            gbuf[tile, i] = gated
        rate = rates_ref[:, lanes]
        far, near = jnp.exp(-float(STEPS - 1) * rate), jnp.exp(-float(STEPS - 2) * rate)
        for r in range(ORDER):
            rows = pl.ds(r, SEGS, stride=ORDER)
            ends[tile, rows, :] = (ends[tile, rows, :] + spread(far[r:r + 1]) * changes[0]
                                   + spread(near[r:r + 1]) * changes[1])
        return carry

    def combine_tile(part):
        def body(tile, carry):
            jump = jnp.exp(-float(STEPS) * rates_ref[:, lanes_of(tile)])
            state = jnp.zeros((ORDER, LANES), F32)
            for seg in range(SEGS):
                inits[tile, pl.ds(seg * ORDER, ORDER), :] = state
                state = jump * state + ends[tile, pl.ds(seg * ORDER, ORDER), :]
            xstate[part, cx, :, lanes_of(tile - part * (TILES // PARTS))] = state
            return carry
        return body

    def row_tile(part):
        def body(tile, carry):
            lanes = lanes_of(tile - part * (TILES // PARTS))
            jump = jnp.exp(-float(ROWS) * rates_ref[:, lanes_of(tile)])
            state = jnp.zeros((ORDER, LANES), F32)
            for position in range(SIDE):
                state = jump * state + xstate[part, position, :, lanes]
            ystate[part, cy, :, lanes] = state
            return carry
        return body

    def seed_tile(part):
        def body(tile, carry):
            lanes = lanes_of(tile - part * (TILES // PARTS))
            rate = rates_ref[:, lanes_of(tile)]
            jump_x = jnp.exp(-float(ROWS) * rate)
            jump_y = jnp.exp(-float(ROWS * SIDE) * rate)
            before_x = jnp.zeros((ORDER, LANES), F32)
            before_y = jnp.zeros((ORDER, LANES), F32)
            for position in range(SIDE - 1):
                before_x = jnp.where(
                    position < cx, jump_x * before_x + xstate[part, position, :, lanes], before_x)
                before_y = jnp.where(
                    position < cy, jump_y * before_y + ystate[part, position, :, lanes], before_y)
            shift = (cx * ROWS).astype(F32)
            state = before_x + jnp.exp(-shift * rate) * before_y
            jump = jnp.exp(-float(STEPS) * rate)
            for seg in range(SEGS):
                rows = pl.ds(seg * ORDER, ORDER)
                inits[tile, rows, :] = inits[tile, rows, :] + state
                state = jump * state
            return carry
        return body

    target_block = jnp.where(role == 0, cz, 2 * SIDE)

    def second_tile(tile, carry):
        lanes = lanes_of(tile)
        decay = [spread(dec[pl.ds(r, 1), lanes]) for r in range(ORDER)]
        weight = [spread(res_ref[pl.ds(r, 1), lanes]) for r in range(ORDER)]
        q_taps = tap_rows(0, lanes)

        def step(i, held):
            q1, q2, states = held
            q0 = strided(0, tile, PAD + i)
            qf = q_taps[0] * q0 + q_taps[1] * q1 + q_taps[2] * q2
            gated = gbuf[tile, i]
            states = tuple(decay[r] * states[r] + gated for r in range(ORDER))
            terms = [weight[r] * states[r] for r in range(ORDER)]
            while len(terms) > 1:
                terms = [terms[j] + terms[j + 1] for j in range(0, len(terms), 2)]
            ybuf[pl.ds(i, SEGS, stride=STEPS), :] = qf * terms[0]
            return q0, q1, states

        start = (strided(0, tile, PAD - 1), strided(0, tile, PAD - 2),
                 tuple(inits[tile, pl.ds(r, SEGS, stride=ORDER), :] for r in range(ORDER)))
        lax.fori_loop(0, STEPS, step, start, unroll=4)
        abuf[target_block, tile // 2, :, lanes_of(tile % 2)] = ybuf[pl.ds(0, ROWS), :].astype(BF16)
        return carry

    def tiles(part, body):
        each = TILES // PARTS
        lax.fori_loop(part * each, (part + 1) * each, body, 0)

    def outputs(q):
        lax.fori_loop(2 * q, 2 * q + 2, second_tile, 0)

    def states_out(part, stage):
        for distance in (2, 1, 3):
            state_copy(part, stage, distance, False).start()

    def states_in(part, stage):
        for distance in (2, 1, 3):
            state_copy(part, stage, distance, True).wait_recv()

    def when(wanted, call, *args):
        @pl.when(role == wanted)
        def _():
            call(*args)

    def a_start(q, *kinds):
        for kind in kinds:
            a_copy(q, kind, False).start()

    def p_begin(q):
        p_copy(q).start()

    def a_cross(q):
        p_copy(q).wait_recv()
        a_start(q, 0, 1, 4)

    def a_middle(q):
        for kind in (0, 1):
            a_copy(q, kind, True).wait_recv()
            a_copy(q, kind + 2, False).start()
            a_copy(q, kind + 5, False).start()

    def a_end(q):
        for kind in (2, 3):
            a_copy(q, kind, True).wait_recv()
        a_copy(q, 7, False).start()

    def a_sibling(q, *kinds):
        for kind in kinds:
            a_copy(q, kind, True).wait_recv()

    def a_pair(q):
        a_sibling(q, 4, 5, 6, 7)

    def product(group, n):
        left = jnp.concatenate(
            [abuf[group * SIDE + block, q] for block in range(SIDE) for q in range(PIECES)], 1)
        right = jnp.concatenate([wbuf[j, n] for j in range(2 * SIDE)], 0)
        return jnp.dot(left, right, preferred_element_type=F32)

    def nearby(centre, n, offsets):
        blocks = [mod(centre + offset) for offset in offsets]
        left = jnp.concatenate(
            [abuf[SIDE + block, q] for block in blocks for q in range(PIECES)], 1)
        right = jnp.concatenate([wbuf[block * 2 + j, n] for block in blocks for j in range(2)], 0)
        return jnp.dot(left, right, preferred_element_type=F32)

    def partial(n):
        cout[n] = product(1, n).astype(BF16)

    def prepare(centre, n):
        early[n] = nearby(centre, n, OFFS[:3])

    def finish(centre, n):
        cout[n] = (early[n] + nearby(centre, n, OFFS[3:])).astype(BF16)

    def own(first, count):
        def body(n, carry):
            acc[n] = product(0, n)
            return carry

        lax.fori_loop(first, first + count, body, 0)

    def c_begin(n):
        c_copy(n).start()

    def c_end(n):
        c_copy(n).wait_recv()
        out_ref[:, pl.ds(n * CHUNK, CHUNK)] = (acc[n] + cin[n].astype(F32)).astype(BF16)

    widen(1)
    widen(2)
    enter()
    w_start(0, 0, 1)
    tiles(0, first_tile)
    widen_halo(1)
    widen_halo(2)
    tiles(0, mend_tile)
    tiles(0, combine_tile(0))
    states_out(0, 0)
    tiles(1, first_tile)
    tiles(1, mend_tile)
    tiles(1, combine_tile(1))
    states_out(1, 0)
    w_start(0, 8, 4)
    widen(0)
    widen_halo(0)
    states_in(0, 0)
    tiles(0, row_tile(0))
    states_out(0, 1)
    states_in(1, 0)
    tiles(1, row_tile(1))
    states_out(1, 1)
    w_start(0, 9, 10)
    w_own(1)
    states_in(0, 1)
    tiles(0, seed_tile(0))
    outputs(0)
    when(1, p_begin, 0)
    when(0, a_start, 0, 0, 1, 4)
    outputs(1)
    when(1, p_begin, 1)
    when(0, a_start, 1, 0, 1, 4)
    states_in(1, 1)
    tiles(1, seed_tile(1))
    outputs(2)
    when(1, p_begin, 2)
    when(0, a_start, 2, 4)
    when(1, a_cross, 0)
    outputs(3)
    when(1, p_begin, 3)
    when(0, a_start, 3, 4)
    when(1, a_cross, 1)
    w_first(0)
    when(1, a_middle, 0)
    when(1, a_cross, 2)
    when(1, a_middle, 1)
    when(1, a_cross, 3)
    when(1, a_end, 0)
    when(1, a_middle, 2)
    w_second(0)
    when(1, a_end, 1)
    when(1, a_middle, 3)
    when(0, a_middle, 0)
    when(0, a_sibling, 3, 4)
    when(0, a_sibling, 0, 4, 5, 6, 7)
    when(0, a_sibling, 1, 4, 5, 6)
    when(0, a_start, 2, 0, 1)
    w_first(1)
    w_own(2)
    when(1, a_end, 2)
    when(1, a_end, 3)
    when(0, a_sibling, 1, 7)
    when(0, a_start, 3, 0, 1)
    w_third(0)
    when(0, a_pair, 2)
    when(0, a_sibling, 3, 5, 6, 7)
    partial(0)
    c_begin(0)
    partial(1)
    c_begin(1)
    when(0, a_middle, 1)
    when(0, a_end, 0)
    w_second(1)
    when(0, a_middle, 2)
    when(0, a_end, 1)
    w_first(2)
    when(0, a_middle, 3)
    w_wait(1, 4, 5, 6)
    prepare(cy, 2)
    w_wait(1, 7, 11, 12, 15, 16)
    finish(cy, 2)
    c_begin(2)
    when(0, a_end, 2)
    when(0, a_end, 3)
    w_second(2)
    w_wait(2, 4, 5, 6)
    prepare(cy, 3)
    w_wait(2, 7, 11, 12, 15, 16)
    finish(cy, 3)
    c_begin(3)
    when(1, a_pair, 0)
    when(1, a_pair, 1)
    when(1, a_pair, 2)
    when(1, a_pair, 3)
    own(0, 4)
    for n in range(CHUNKS):
        c_end(n)

    for n in range(len(GROUPS)):
        for number in range(PER_GROUP):
            w_copy(n, number, False).wait_send()
    for n in range(CHUNKS):
        c_copy(n).wait_send()
    for q in range(PIECES):
        for kind in range(8):
            a_copy(q, kind, False).wait_send()
    for q in range(PARTS):
        for stage in range(2):
            for distance in (1, 2, 3):
                state_copy(q, stage, distance, False).wait_send()

    @pl.when(role == 1)
    def _():
        for q in range(PIECES):
            p_copy(q).wait_send()

    for index in range(3):
        halo_copy(index).wait_send()


def per_device(query, keys_in, values_in, short_taps, mode_rates, mode_residues, out_weight):
    vmem = pl.BlockSpec(memory_space=pltpu.VMEM)
    hbm = pl.BlockSpec(memory_space=pl.ANY)
    dma = pltpu.SemaphoreType.DMA
    return pl.pallas_call(
        kernel,
        out_shape=jax.ShapeDtypeStruct((ROWS, WIDTH), BF16),
        in_specs=[hbm] * 3 + [vmem] * 3 + [hbm],
        out_specs=vmem,
        scratch_shapes=[
            pltpu.VMEM((2 * SIDE, CHUNKS, ROWS, CHUNK), BF16),
            pltpu.VMEM((2 * SIDE + 1, PIECES, ROWS, PIECE), BF16),
            pltpu.VMEM((CHUNKS, ROWS, CHUNK), F32),
            pltpu.VMEM((CHUNKS, ROWS, CHUNK), F32),
            pltpu.VMEM((CHUNKS, ROWS, CHUNK), BF16),
            pltpu.VMEM((CHUNKS, ROWS, CHUNK), BF16),
            pltpu.VMEM((3, ROWS, WIDTH), BF16),
            pltpu.VMEM((3, TILES, PAD + ROWS + STEPS, LANES), F32),
            pltpu.VMEM((TILES, STEPS, SEGS, LANES), F32),
            pltpu.VMEM((ROWS + STEPS, LANES), F32),
            pltpu.VMEM((3, HALO, WIDTH), BF16),
            pltpu.VMEM((ORDER, WIDTH), F32),
            pltpu.VMEM((TILES, (SEGS + 1) * ORDER, LANES), F32),
            pltpu.VMEM((TILES, (SEGS + 1) * ORDER, LANES), F32),
            pltpu.VMEM((PARTS, SIDE, ORDER, PART), F32),
            pltpu.VMEM((PARTS, SIDE, ORDER, PART), F32),
            dma((len(GROUPS) * PER_GROUP,)), dma((len(GROUPS) * PER_GROUP,)),
            dma((PIECES * 8,)), dma((PIECES * 8,)), dma((PIECES,)), dma((PIECES,)),
            dma((CHUNKS,)), dma((CHUNKS,)), dma((3,)), dma((3,)),
            dma((PARTS * 6,)), dma((PARTS * 6,)), dma((CHUNKS,)), dma((3,)),
        ],
        compiler_params=pltpu.CompilerParams(
            collective_id=0, has_side_effects=True, vmem_limit_bytes=56 * 1024 * 1024),
        cost_estimate=pl.CostEstimate(
            flops=2 * ROWS * 8192 * WIDTH, bytes_accessed=6 * 1024 * 1024, transcendentals=0),
    )(query, keys_in, values_in, short_taps, mode_rates, mode_residues, out_weight)


def solution(mesh):
    in_specs = (
        P("ctx", "ch"),
        P("ctx", "ch"),
        P("ctx", "ch"),
        P(None, None, "ch"),
        P(None, "ch"),
        P(None, "ch"),
        P("ctx", "ch"),
    )
    return jax.shard_map(
        per_device, mesh=mesh, in_specs=in_specs, out_specs=P("ctx", "ch"), check_vma=False
    )
```

```python
import jax
import jax.numpy as jnp
from jax import lax
from jax.experimental import pallas as pl
from jax.experimental.pallas import tpu as pltpu
from jax.sharding import PartitionSpec as P

MESH = pl.DeviceIdType.MESH
SIDE = 4
ORDER = 16
ROWS = 512
WIDTH = 1024
LANES = 128
TILES = WIDTH // LANES
SEGS = 8
STEPS = ROWS // SEGS
PAD = 8
HALO = 16
PARTS = 2
PART = WIDTH // PARTS
PIECES = 4
PIECE = WIDTH // PIECES
CHUNKS = 4
CHUNK = WIDTH // CHUNKS
CUT = 224
OFFS = (0, -1, 1, 2)
PER_GROUP = 17
GROUPS = ((0, 2), (2, 1), (3, 1))
F32 = jnp.float32
BF16 = jnp.bfloat16


def kernel(
    q_hbm, k_hbm, v_hbm, taps_ref, rates_ref, res_ref, w_ref, out_ref,
    wbuf, abuf, acc, early, cout, cin, inputs, streams, gbuf, ybuf, halo, dec, ends, inits, xstate, ystate,
    w_send, w_recv, a_send, a_recv, p_send, p_recv, c_send, c_recv, h_send, h_recv, s_send, s_recv,
    own_sem, in_sem,
):
    ctx = lax.axis_index("ctx")
    ch = lax.axis_index("ch")
    cy, cx = ctx // SIDE, ctx % SIDE
    cz, core = ch // 2, ch % 2
    column, side = cx % 2, cx // 2
    role = jnp.where(core == side, 0, 1)

    def mod(value):
        return lax.rem(value + 2 * SIDE, SIDE)

    def at_xy(y, x):
        return (mod(y) * SIDE + mod(x), ch)

    following = (lax.rem(ctx + 1, SIDE * SIDE), ch)
    previous = (lax.rem(ctx + SIDE * SIDE - 1, SIDE * SIDE), ch)
    sibling = (ctx, cz * 2 + 1 - core)
    beside = at_xy(cy, cx + 1 - 2 * column)
    partner = at_xy(cy, 3 - cx)
    crossed = (cy * SIDE + 3 - cx, cz * 2 + 1 - core)

    def at_z(z):
        return (ctx, mod(z) * 2 + core)

    barrier = pltpu.get_barrier_semaphore()
    others = [at_xy(cy, cx + d) for d in (1, 2, 3)] + [at_xy(cy + d, cx) for d in (1, 2, 3)]
    others += [at_z(cz + 1), at_z(cz - 1), sibling, following, previous, crossed]
    for other in others:
        pl.semaphore_signal(barrier, inc=1, device_id=other, device_id_type=MESH)

    sources = (q_hbm, k_hbm, v_hbm)

    def own_copy(n):
        return pltpu.make_async_copy(
            w_ref.at[:, pl.ds(n * CHUNK, CHUNK)], wbuf.at[cy * 2 + column, n], own_sem.at[n])

    def in_copy(index):
        return pltpu.make_async_copy(sources[index], inputs.at[index], in_sem.at[index])

    for n in range(CHUNKS):
        own_copy(n).start()
    for index in (1, 2, 0):
        in_copy(index).start()
    def halo_copy(index):
        return pltpu.make_async_remote_copy(
            src_ref=sources[index].at[pl.ds(ROWS - HALO, HALO)], dst_ref=halo.at[index],
            send_sem=h_send.at[index], recv_sem=h_recv.at[index],
            device_id=following, device_id_type=MESH)

    def enter():
        pl.semaphore_wait(barrier, len(others))
        for index in (1, 2, 0):
            halo_copy(index).start()
        for n in range(CHUNKS):
            own_copy(n).wait()

    def ring(kind, receiving):
        step = 1 if kind % 2 == 0 else -1
        if receiving:
            return step, (-step if kind < 2 else -2 * step)
        return step, (0 if kind < 2 else -step)

    def w_copy(n, number, receiving):
        if number < 4 or number >= 9:
            kind = number if number < 4 else (number - 9) % 4
            step, back = ring(kind, receiving)
            row = cy + back
            flip = number >= 13
            target = at_xy(cy + step, cx)
            low, high = (0, CUT) if number < 4 else (CUT, ROWS)
            middle = (low + high) // 2
            if kind == 2:
                high = middle
            if kind == 3:
                low = middle
        else:
            row = cy + (OFFS[number - 4] if number < 8 else 0)
            flip = receiving
            target = beside
            low, high = (0, CUT) if number < 8 else (CUT, ROWS)
        across = 1 - column if flip else column
        where = wbuf.at[mod(row) * 2 + across, pl.ds(*GROUPS[n]), pl.ds(low, high - low)]
        index = n * PER_GROUP + number
        return pltpu.make_async_remote_copy(
            src_ref=where, dst_ref=where, send_sem=w_send.at[index], recv_sem=w_recv.at[index],
            device_id=target, device_id_type=MESH)

    def w_start(n, *numbers):
        for number in numbers:
            w_copy(n, number, False).start()

    def w_wait(n, *numbers):
        for number in numbers:
            w_copy(n, number, True).wait_recv()

    def w_own(n):
        w_start(n, 8, 0, 1, 9, 10, 4)

    def w_first(n):
        w_wait(n, 8)
        w_start(n, 13, 14)
        for kind in (0, 1):
            w_wait(n, kind)
            w_start(n, kind + 2, 5 + kind)
        for kind in (0, 1):
            w_wait(n, 9 + kind)
            w_start(n, 11 + kind)

    def w_second(n):
        w_wait(n, 2, 3)
        w_start(n, 7)
        for kind in (0, 1):
            w_wait(n, 13 + kind)
            w_start(n, 15 + kind)

    def w_third(n):
        w_wait(n, 4, 5, 6, 7, 11, 12, 15, 16)

    def a_copy(q, kind, receiving):
        low, size = 0, ROWS
        held = role
        if kind < 4:
            step, back = ring(kind, receiving)
            if kind >= 2:
                low, size = (ROWS // 2 if kind == 3 else 0), ROWS // 2
            target = at_z(cz + step)
        else:
            back = OFFS[kind - 4]
            held = 1 - role if receiving else role
            target = sibling
        where = abuf.at[held * SIDE + mod(cz + back), q, pl.ds(low, size)]
        index = q * 8 + kind
        return pltpu.make_async_remote_copy(
            src_ref=where, dst_ref=where, send_sem=a_send.at[index], recv_sem=a_recv.at[index],
            device_id=target, device_id_type=MESH)

    def p_copy(q):
        return pltpu.make_async_remote_copy(
            src_ref=abuf.at[2 * SIDE, q], dst_ref=abuf.at[SIDE + cz, q],
            send_sem=p_send.at[q], recv_sem=p_recv.at[q],
            device_id=crossed, device_id_type=MESH)

    def c_copy(n):
        return pltpu.make_async_remote_copy(
            src_ref=cout.at[n], dst_ref=cin.at[n], send_sem=c_send.at[n], recv_sem=c_recv.at[n],
            device_id=partner, device_id_type=MESH)

    def state_copy(part, stage, distance, receiving):
        held = (xstate, ystate)[stage]
        position = (cx, cy)[stage]
        index = mod(position - distance) if receiving else position
        target = at_xy(cy, cx + distance) if stage == 0 else at_xy(cy + distance, cx)
        number = part * 6 + stage * 3 + distance - 1
        where = held.at[part, index]
        return pltpu.make_async_remote_copy(
            src_ref=where, dst_ref=where,
            send_sem=s_send.at[number], recv_sem=s_recv.at[number],
            device_id=target, device_id_type=MESH)


    dec[...] = jnp.exp(-rates_ref[...])

    def lanes_of(tile):
        return pl.ds(pl.multiple_of(tile * LANES, LANES), LANES)

    def widen(index):
        in_copy(index).wait()

        def body(tile, carry):
            streams[index, tile, pl.ds(0, PAD), :] = jnp.zeros((PAD, LANES), F32)
            streams[index, tile, pl.ds(PAD, ROWS), :] = inputs[index, :, lanes_of(tile)].astype(F32)
            return carry

        lax.fori_loop(0, TILES, body, 0)

    def widen_halo(index):
        halo_copy(index).wait_recv()
        keep = jnp.where(ctx > 0, 1.0, 0.0).astype(F32)

        def body(tile, carry):
            rim = halo[index, :, lanes_of(tile)].astype(F32)
            streams[index, tile, pl.ds(0, PAD), :] = rim[HALO - PAD:] * keep
            return carry

        lax.fori_loop(0, TILES, body, 0)

    def spread(row):
        return jnp.broadcast_to(row, (SEGS, LANES))

    def strided(index, tile, start):
        return streams[index, tile, pl.ds(start, SEGS, stride=STEPS), :]

    def tap_rows(index, lanes):
        return [spread(taps_ref[index, pl.ds(j, 1), lanes]) for j in range(3)]

    def gate(k_taps, v_taps, k0, k1, k2, v0, v1, v2):
        kf = k_taps[0] * k0 + k_taps[1] * k1 + k_taps[2] * k2
        vf = v_taps[0] * v0 + v_taps[1] * v1 + v_taps[2] * v2
        return kf * vf

    def first_tile(tile, carry):
        lanes = lanes_of(tile)
        decay = [spread(dec[pl.ds(r, 1), lanes]) for r in range(ORDER)]
        k_taps, v_taps = tap_rows(1, lanes), tap_rows(2, lanes)

        def step(i, held):
            k1, k2, v1, v2, states = held
            k0, v0 = strided(1, tile, PAD + i), strided(2, tile, PAD + i)
            gated = gate(k_taps, v_taps, k0, k1, k2, v0, v1, v2)
            gbuf[tile, i] = gated
            states = tuple(decay[r] * states[r] + gated for r in range(ORDER))
            return k0, k1, v0, v1, states

        zero = jnp.zeros((SEGS, LANES), F32)
        start = (strided(1, tile, PAD - 1), strided(1, tile, PAD - 2),
                 strided(2, tile, PAD - 1), strided(2, tile, PAD - 2), (zero,) * ORDER)
        states = lax.fori_loop(0, STEPS, step, start, unroll=8)[4]
        for r in range(ORDER):
            ends[tile, pl.ds(r, SEGS, stride=ORDER), :] = states[r]
        return carry

    def mend_tile(tile, carry):
        lanes = lanes_of(tile)
        k_taps, v_taps = tap_rows(1, lanes), tap_rows(2, lanes)
        k = [strided(1, tile, PAD + d) for d in (-2, -1, 0, 1)]
        v = [strided(2, tile, PAD + d) for d in (-2, -1, 0, 1)]
        changes = []
        for i in (0, 1):
            gated = gate(k_taps, v_taps, k[i + 2], k[i + 1], k[i], v[i + 2], v[i + 1], v[i])
            changes.append(gated - gbuf[tile, i])
            gbuf[tile, i] = gated
        rate = rates_ref[:, lanes]
        far, near = jnp.exp(-float(STEPS - 1) * rate), jnp.exp(-float(STEPS - 2) * rate)
        for r in range(ORDER):
            rows = pl.ds(r, SEGS, stride=ORDER)
            ends[tile, rows, :] = (ends[tile, rows, :] + spread(far[r:r + 1]) * changes[0]
                                   + spread(near[r:r + 1]) * changes[1])
        return carry

    def combine_tile(part):
        def body(tile, carry):
            jump = jnp.exp(-float(STEPS) * rates_ref[:, lanes_of(tile)])
            state = jnp.zeros((ORDER, LANES), F32)
            for seg in range(SEGS):
                inits[tile, pl.ds(seg * ORDER, ORDER), :] = state
                state = jump * state + ends[tile, pl.ds(seg * ORDER, ORDER), :]
            xstate[part, cx, :, lanes_of(tile - part * (TILES // PARTS))] = state
            return carry
        return body

    def row_tile(part):
        def body(tile, carry):
            lanes = lanes_of(tile - part * (TILES // PARTS))
            jump = jnp.exp(-float(ROWS) * rates_ref[:, lanes_of(tile)])
            state = jnp.zeros((ORDER, LANES), F32)
            for position in range(SIDE):
                state = jump * state + xstate[part, position, :, lanes]
            ystate[part, cy, :, lanes] = state
            return carry
        return body

    def seed_tile(part):
        def body(tile, carry):
            lanes = lanes_of(tile - part * (TILES // PARTS))
            rate = rates_ref[:, lanes_of(tile)]
            jump_x = jnp.exp(-float(ROWS) * rate)
            jump_y = jnp.exp(-float(ROWS * SIDE) * rate)
            before_x = jnp.zeros((ORDER, LANES), F32)
            before_y = jnp.zeros((ORDER, LANES), F32)
            for position in range(SIDE - 1):
                before_x = jnp.where(
                    position < cx, jump_x * before_x + xstate[part, position, :, lanes], before_x)
                before_y = jnp.where(
                    position < cy, jump_y * before_y + ystate[part, position, :, lanes], before_y)
            shift = (cx * ROWS).astype(F32)
            state = before_x + jnp.exp(-shift * rate) * before_y
            jump = jnp.exp(-float(STEPS) * rate)
            for seg in range(SEGS):
                rows = pl.ds(seg * ORDER, ORDER)
                inits[tile, rows, :] = inits[tile, rows, :] + state
                state = jump * state
            return carry
        return body

    target_block = jnp.where(role == 0, cz, 2 * SIDE)

    def second_tile(tile, carry):
        lanes = lanes_of(tile)
        decay = [spread(dec[pl.ds(r, 1), lanes]) for r in range(ORDER)]
        weight = [spread(res_ref[pl.ds(r, 1), lanes]) for r in range(ORDER)]
        q_taps = tap_rows(0, lanes)

        def step(i, held):
            q1, q2, states = held
            q0 = strided(0, tile, PAD + i)
            qf = q_taps[0] * q0 + q_taps[1] * q1 + q_taps[2] * q2
            gated = gbuf[tile, i]
            states = tuple(decay[r] * states[r] + gated for r in range(ORDER))
            terms = [weight[r] * states[r] for r in range(ORDER)]
            while len(terms) > 1:
                terms = [terms[j] + terms[j + 1] for j in range(0, len(terms), 2)]
            ybuf[pl.ds(i, SEGS, stride=STEPS), :] = qf * terms[0]
            return q0, q1, states

        start = (strided(0, tile, PAD - 1), strided(0, tile, PAD - 2),
                 tuple(inits[tile, pl.ds(r, SEGS, stride=ORDER), :] for r in range(ORDER)))
        lax.fori_loop(0, STEPS, step, start, unroll=8)
        abuf[target_block, tile // 2, :, lanes_of(tile % 2)] = ybuf[pl.ds(0, ROWS), :].astype(BF16)
        return carry

    def tiles(part, body):
        each = TILES // PARTS
        lax.fori_loop(part * each, (part + 1) * each, body, 0)

    def outputs(q):
        lax.fori_loop(2 * q, 2 * q + 2, second_tile, 0)

    def states_out(part, stage):
        for distance in (2, 1, 3):
            state_copy(part, stage, distance, False).start()

    def states_in(part, stage):
        for distance in (2, 1, 3):
            state_copy(part, stage, distance, True).wait_recv()

    def when(wanted, call, *args):
        @pl.when(role == wanted)
        def _():
            call(*args)

    def a_start(q, *kinds):
        for kind in kinds:
            a_copy(q, kind, False).start()

    def p_begin(q):
        p_copy(q).start()

    def a_cross(q):
        p_copy(q).wait_recv()
        a_start(q, 0, 1, 4)

    def a_middle(q):
        for kind in (0, 1):
            a_copy(q, kind, True).wait_recv()
            a_copy(q, kind + 2, False).start()
            a_copy(q, kind + 5, False).start()

    def a_end(q):
        for kind in (2, 3):
            a_copy(q, kind, True).wait_recv()
        a_copy(q, 7, False).start()

    def a_sibling(q, *kinds):
        for kind in kinds:
            a_copy(q, kind, True).wait_recv()

    def a_pair(q):
        a_sibling(q, 4, 5, 6, 7)

    def product(group, n):
        left = jnp.concatenate(
            [abuf[group * SIDE + block, q] for block in range(SIDE) for q in range(PIECES)], 1)
        right = jnp.concatenate([wbuf[j, n] for j in range(2 * SIDE)], 0)
        return jnp.dot(left, right, preferred_element_type=F32)

    def nearby(centre, n, offsets):
        blocks = [mod(centre + offset) for offset in offsets]
        left = jnp.concatenate(
            [abuf[SIDE + block, q] for block in blocks for q in range(PIECES)], 1)
        right = jnp.concatenate([wbuf[block * 2 + j, n] for block in blocks for j in range(2)], 0)
        return jnp.dot(left, right, preferred_element_type=F32)

    def partial(n):
        cout[n] = product(1, n).astype(BF16)

    def prepare(centre, n):
        early[n] = nearby(centre, n, OFFS[:3])

    def finish(centre, n):
        cout[n] = (early[n] + nearby(centre, n, OFFS[3:])).astype(BF16)

    def own(first, count):
        def body(n, carry):
            acc[n] = product(0, n)
            return carry

        lax.fori_loop(first, first + count, body, 0)

    def c_begin(n):
        c_copy(n).start()

    def c_end(n):
        c_copy(n).wait_recv()
        out_ref[:, pl.ds(n * CHUNK, CHUNK)] = (acc[n] + cin[n].astype(F32)).astype(BF16)

    widen(1)
    widen(2)
    enter()
    w_start(0, 0, 1)
    tiles(0, first_tile)
    widen_halo(1)
    widen_halo(2)
    tiles(0, mend_tile)
    tiles(0, combine_tile(0))
    states_out(0, 0)
    tiles(1, first_tile)
    tiles(1, mend_tile)
    tiles(1, combine_tile(1))
    states_out(1, 0)
    w_start(0, 8, 4)
    widen(0)
    widen_halo(0)
    states_in(0, 0)
    tiles(0, row_tile(0))
    states_out(0, 1)
    states_in(1, 0)
    tiles(1, row_tile(1))
    states_out(1, 1)
    w_start(0, 9, 10)
    w_own(1)
    states_in(0, 1)
    tiles(0, seed_tile(0))
    outputs(0)
    when(1, p_begin, 0)
    when(0, a_start, 0, 0, 1, 4)
    outputs(1)
    when(1, p_begin, 1)
    when(0, a_start, 1, 0, 1, 4)
    states_in(1, 1)
    tiles(1, seed_tile(1))
    outputs(2)
    when(1, p_begin, 2)
    when(0, a_start, 2, 4)
    when(1, a_cross, 0)
    outputs(3)
    when(1, p_begin, 3)
    when(0, a_start, 3, 4)
    when(1, a_cross, 1)
    w_first(0)
    when(1, a_middle, 0)
    when(1, a_cross, 2)
    when(1, a_middle, 1)
    when(1, a_cross, 3)
    when(1, a_end, 0)
    when(1, a_middle, 2)
    w_second(0)
    when(1, a_end, 1)
    when(1, a_middle, 3)
    when(0, a_middle, 0)
    when(0, a_sibling, 3, 4)
    when(0, a_sibling, 0, 4, 5, 6, 7)
    when(0, a_sibling, 1, 4, 5, 6)
    when(0, a_start, 2, 0, 1)
    w_first(1)
    w_own(2)
    when(1, a_end, 2)
    when(1, a_end, 3)
    when(0, a_sibling, 1, 7)
    when(0, a_start, 3, 0, 1)
    w_third(0)
    when(0, a_pair, 2)
    when(0, a_sibling, 3, 5, 6, 7)
    partial(0)
    c_begin(0)
    partial(1)
    c_begin(1)
    when(0, a_middle, 1)
    when(0, a_end, 0)
    w_second(1)
    when(0, a_middle, 2)
    when(0, a_end, 1)
    w_first(2)
    when(0, a_middle, 3)
    w_wait(1, 4, 5, 6)
    prepare(cy, 2)
    w_wait(1, 7, 11, 12, 15, 16)
    finish(cy, 2)
    c_begin(2)
    when(0, a_end, 2)
    when(0, a_end, 3)
    w_second(2)
    w_wait(2, 4, 5, 6)
    prepare(cy, 3)
    w_wait(2, 7, 11, 12, 15, 16)
    finish(cy, 3)
    c_begin(3)
    when(1, a_pair, 0)
    when(1, a_pair, 1)
    when(1, a_pair, 2)
    when(1, a_pair, 3)
    own(0, 4)
    for n in range(CHUNKS):
        c_end(n)

    for n in range(len(GROUPS)):
        for number in range(PER_GROUP):
            w_copy(n, number, False).wait_send()
    for n in range(CHUNKS):
        c_copy(n).wait_send()
    for q in range(PIECES):
        for kind in range(8):
            a_copy(q, kind, False).wait_send()
    for q in range(PARTS):
        for stage in range(2):
            for distance in (1, 2, 3):
                state_copy(q, stage, distance, False).wait_send()

    @pl.when(role == 1)
    def _():
        for q in range(PIECES):
            p_copy(q).wait_send()

    for index in range(3):
        halo_copy(index).wait_send()


def per_device(query, keys_in, values_in, short_taps, mode_rates, mode_residues, out_weight):
    vmem = pl.BlockSpec(memory_space=pltpu.VMEM)
    hbm = pl.BlockSpec(memory_space=pl.ANY)
    dma = pltpu.SemaphoreType.DMA
    return pl.pallas_call(
        kernel,
        out_shape=jax.ShapeDtypeStruct((ROWS, WIDTH), BF16),
        in_specs=[hbm] * 3 + [vmem] * 3 + [hbm],
        out_specs=vmem,
        scratch_shapes=[
            pltpu.VMEM((2 * SIDE, CHUNKS, ROWS, CHUNK), BF16),
            pltpu.VMEM((2 * SIDE + 1, PIECES, ROWS, PIECE), BF16),
            pltpu.VMEM((CHUNKS, ROWS, CHUNK), F32),
            pltpu.VMEM((CHUNKS, ROWS, CHUNK), F32),
            pltpu.VMEM((CHUNKS, ROWS, CHUNK), BF16),
            pltpu.VMEM((CHUNKS, ROWS, CHUNK), BF16),
            pltpu.VMEM((3, ROWS, WIDTH), BF16),
            pltpu.VMEM((3, TILES, PAD + ROWS + STEPS, LANES), F32),
            pltpu.VMEM((TILES, STEPS, SEGS, LANES), F32),
            pltpu.VMEM((ROWS + STEPS, LANES), F32),
            pltpu.VMEM((3, HALO, WIDTH), BF16),
            pltpu.VMEM((ORDER, WIDTH), F32),
            pltpu.VMEM((TILES, (SEGS + 1) * ORDER, LANES), F32),
            pltpu.VMEM((TILES, (SEGS + 1) * ORDER, LANES), F32),
            pltpu.VMEM((PARTS, SIDE, ORDER, PART), F32),
            pltpu.VMEM((PARTS, SIDE, ORDER, PART), F32),
            dma((len(GROUPS) * PER_GROUP,)), dma((len(GROUPS) * PER_GROUP,)),
            dma((PIECES * 8,)), dma((PIECES * 8,)), dma((PIECES,)), dma((PIECES,)),
            dma((CHUNKS,)), dma((CHUNKS,)), dma((3,)), dma((3,)),
            dma((PARTS * 6,)), dma((PARTS * 6,)), dma((CHUNKS,)), dma((3,)),
        ],
        compiler_params=pltpu.CompilerParams(
            collective_id=0, has_side_effects=True, vmem_limit_bytes=56 * 1024 * 1024),
        cost_estimate=pl.CostEstimate(
            flops=2 * ROWS * 8192 * WIDTH, bytes_accessed=6 * 1024 * 1024, transcendentals=0),
    )(query, keys_in, values_in, short_taps, mode_rates, mode_residues, out_weight)


def solution(mesh):
    in_specs = (
        P("ctx", "ch"),
        P("ctx", "ch"),
        P("ctx", "ch"),
        P(None, None, "ch"),
        P(None, "ch"),
        P(None, "ch"),
        P("ctx", "ch"),
    )
    return jax.shard_map(
        per_device, mesh=mesh, in_specs=in_specs, out_specs=P("ctx", "ch"), check_vma=False
    )
```
